256 devices in a mesh: row: 4 (over y), col: 8 (over z), lag: 8 (over x, core).
Axes of the slice: x: 4, y: 4, z: 8, core: 2. Of those that a mesh axis runs over, the one named last changes fastest.
Arguments:
- history: float32 [32, 256, 128], P(None, ('row', 'col', 'lag')), may hold values from -6 to 6
- step_index: int32 [1], replicated, may hold values from 0 to 31
- pair_rows: int32 [4, 8, 32], P('row', 'col'), may hold values from 0 to 63, as said below
- pair_cols: int32 [4, 8, 32], P('row', 'col'), may hold values from 0 to 31, as said below
- lag_pattern: int32 [4, 8, 32, 32], P('row', 'col', None, 'lag'), may hold values 0 or 1
- blocks: float32 [4, 8, 32, 32, 128, 128], P('row', 'col', None, 'lag'), may hold values from -0.1875 to 0.1875
- incident: float32 [256, 128], P(('row', 'col', 'lag')), may hold values from -6 to 6
- self_inverse: float32 [256, 128, 128], P(('row', 'col', 'lag')), may hold values from -0.5 to 0.5
Outputs:
- new_field: float32 [256, 128], P(('row', 'col', 'lag'))
The draws below stay inside these ranges and needn't reach their ends.
Inputs may be any that keep to these rules, and one draw needn't show every extreme that they name: pair_rows[r, c, p] and pair_cols[r, c, p] name a pair whose row block i and column block j (as in the reference program) satisfy i <= j; pairs may repeat. `pair_cols`: see pair_rows.
All inputs are finite; a program needn't handle non-finite values. No bound on the sum of `lag_pattern` on one device may be relied on, other than what follows from the above.
Results may differ from the reference program's by a relative error of at most 0.0003.
Values sent between devices are 32-bit elements; how exact they have to be, the bound alone decides.
No kernel may reach another device: no remote copies, remote signals or barrier semaphores. Data moves between devices by JAX's collectives and lax.ppermute only.
A program may use at most 64 MiB of HBM per device.

```python
import jax
import jax.numpy as jnp
from jax import lax

BLOCK = 128
BLK_DEV = 1
PAIRS_DEV = 32
LAGS = 32
NBLK = 256
GROUP = 8
BAND = 64
N_ROW = 4
N_COL = 8
N_LAG = 8


def pair_helper(key):
    key_row, key_col, key_inner = jax.random.split(key, 3)
    shape = (N_ROW, N_COL, PAIRS_DEV)
    row_index = jnp.broadcast_to(jnp.arange(N_ROW, dtype=jnp.int32)[:, None, None], shape)
    col_index = jnp.broadcast_to(jnp.arange(N_COL, dtype=jnp.int32)[None, :, None], shape)
    slot_index = jnp.broadcast_to(jnp.arange(PAIRS_DEV, dtype=jnp.int32)[None, None, :], shape)
    group_size = BLK_DEV * N_LAG
    row_band = group_size * N_COL
    offset = jax.random.randint(key_row, shape, 0, N_ROW - row_index)
    band_row = row_index + offset
    inner = jax.random.randint(key_col, shape, 0, group_size)
    band_row = jnp.where(slot_index == 0, N_ROW - 1, band_row)
    inner = jnp.where(slot_index == 0, group_size - 1, inner)
    col_local = band_row * group_size + inner
    col_global = band_row * row_band + col_index * group_size + inner
    limit = jnp.minimum(row_band, col_global - row_index * row_band + 1)
    row_local = jax.random.randint(key_inner, shape, 0, limit)
    row_local = jnp.where(slot_index == 0, limit - 1, row_local)
    return (row_local.astype(jnp.int32), col_local.astype(jnp.int32))


def draw_pair_rows(key, part):
    return pair_helper(key)[0]


def draw_pair_cols(key, part):
    return pair_helper(key)[1]


def place_ends(array, stream_key, smallest, top_value):
    longest = array.shape.index(max(array.shape))
    spots = []
    for shift in (0, 1):
        where = [jax.random.randint(jax.random.fold_in(stream_key, axis), (), 0, length) for axis, length in enumerate(array.shape)]
        where[longest] = (where[longest] + shift) % array.shape[longest]
        spots.append(tuple(where))
    return array.at[spots[0]].set(smallest).at[spots[1]].set(top_value)


def block_scale(key, dims, cuts, least, high):
    factor_of, own = 1.0, jax.random.fold_in(key, 6)
    for dim, shards_of in cuts:
        steps = jnp.exp(jax.random.uniform(jax.random.fold_in(own, dim), (shards_of,), jnp.float32, least / len(cuts), high / len(cuts)))
        factor_of = factor_of * jnp.repeat(steps, dims[dim] // shards_of).reshape([-1 if axis == dim else 1 for axis in range(len(dims))])
    return factor_of


def scatter_about(stream_key, dims, deviation, reach, shards=(), held_as=jnp.bfloat16):
    factor_of = block_scale(stream_key, dims, shards, -0.22, 0.18) if shards else 1.0
    values = jax.random.normal(stream_key, dims, jnp.float32) * deviation * factor_of
    return jnp.minimum(jnp.maximum(values, -reach), reach).astype(held_as)


def setup_inputs(seed: int = 0) -> dict:
    streams_of = jax.random.split(jax.random.key(seed), 9)
    return {
        "history": scatter_about(streams_of[0], (LAGS, NBLK, BLOCK), 1.0, 6.0, ((1, 256),), jnp.float32),
        "step_index": jax.random.randint(streams_of[1], (1,), 0, LAGS).astype(jnp.int32),
        "pair_rows": draw_pair_rows(jax.random.fold_in(streams_of[8], 71), 0),
        "pair_cols": draw_pair_cols(jax.random.fold_in(streams_of[8], 71), 0),
        "lag_pattern": place_ends((jax.random.randint(streams_of[4], (N_ROW, N_COL, PAIRS_DEV, LAGS), 0, 2) < 1).astype(jnp.int32), jax.random.fold_in(streams_of[4], 1), 0, 1),
        "blocks": scatter_about(streams_of[5], (N_ROW, N_COL, PAIRS_DEV, LAGS, BLOCK, BLOCK), (8 * BLOCK) ** -0.5, 0.1875, ((0, 4), (1, 8), (3, 8)), jnp.float32),
        "incident": scatter_about(streams_of[6], (NBLK, BLOCK), 1.0, 6.0, ((0, 256),), jnp.float32),
        "self_inverse": scatter_about(streams_of[7], (NBLK, BLOCK, BLOCK), BLOCK ** -0.5, 0.5, ((0, 256),), jnp.float32),
    }


def reference(history, step_index, pair_rows, pair_cols, lag_pattern, blocks, incident, self_inverse):
    lag_ids = jnp.arange(LAGS, dtype=jnp.int32)
    slot_ids = jnp.mod(step_index[0] - 1 - lag_ids, LAGS).astype(jnp.int32)
    past = jnp.take(history, slot_ids, axis=0)
    row_band = BAND
    group_size = GROUP
    row_index = jnp.arange(N_ROW, dtype=jnp.int32)[:, None, None]
    col_index = jnp.arange(N_COL, dtype=jnp.int32)[None, :, None]
    row_global = (row_index * row_band + pair_rows).reshape(-1).astype(jnp.int32)
    col_global = ((pair_cols // group_size) * row_band + col_index * group_size + pair_cols % group_size).reshape(-1).astype(jnp.int32)
    matrices = blocks.reshape(-1, LAGS, BLOCK, BLOCK)
    lag_masks = lag_pattern.reshape(-1, LAGS).astype(jnp.float32)

    def visit_pair(convolved, pair_item):
        row_block, col_block, matrix, lag_mask = pair_item
        row_source = jnp.take(past, row_block, axis=1)
        col_source = jnp.take(past, col_block, axis=1)
        forward = jnp.einsum('lab,lb,l->a', matrix, col_source, lag_mask, precision=lax.Precision.HIGHEST)
        mirror = jnp.einsum('lab,la,l->b', matrix, row_source, lag_mask, precision=lax.Precision.HIGHEST)
        mirror = mirror * jnp.where(row_block != col_block, 1.0, 0.0).astype(jnp.float32)
        convolved = convolved.at[row_block].add(forward)
        convolved = convolved.at[col_block].add(mirror)
        return convolved, None

    start = jnp.zeros((NBLK, BLOCK), jnp.float32)
    convolved = lax.scan(visit_pair, start, (row_global, col_global, matrices, lag_masks))[0]
    return jnp.einsum('bxy,by->bx', self_inverse, incident - convolved, precision=lax.Precision.HIGHEST)
```

```python
import functools

import jax
import jax.numpy as jnp
from jax import lax
from jax.experimental import pallas as pl
from jax.experimental.pallas import tpu as pltpu
from jax.sharding import PartitionSpec as P

VMEM = pl.BlockSpec(memory_space=pltpu.VMEM)
SMEM = pl.BlockSpec(memory_space=pltpu.SMEM)


def order_kernel(lags, copies, step_ref, hist_ref, send_ref, past_ref):
    first = step_ref[0] - 1 + lags
    for g in range(lags):
        slot = lax.rem(first - g, lags)
        row = hist_ref[pl.ds(slot, 1), :]
        past_ref[pl.ds(g, 1), :] = row
        for k in range(copies):
            send_ref[pl.ds(k * lags + g, 1), :] = row


def forward_kernel(pairs, lag_local, n_lag, rows_ref, cols_ref, mask_ref, mats_ref, src_ref, past_ref, out_ref):
    lanes = lax.broadcasted_iota(jnp.int32, (128, 128), 1)

    def body(p, total):
        col = cols_ref[p]
        acc = jnp.zeros((128, 128), jnp.float32)
        for l in range(lag_local):
            keep = mask_ref[p, l] != 0
            vec = src_ref[pl.ds(col * lag_local + l, 1), :]
            acc = acc + mats_ref[p * lag_local + l] * jnp.where(keep, vec, 0.0)
        sums = jnp.sum(acc, axis=1, keepdims=True)
        return total + jnp.where(lanes == rows_ref[p], sums, 0.0)

    total = lax.fori_loop(0, pairs, body, jnp.zeros((128, 128), jnp.float32))
    chunk = lag_local + 1
    dests = out_ref.shape[0] // chunk
    out_ref[pl.ds(lag_local, dests, stride=chunk), :] = total.T[:dests]
    for d in range(dests):
        first = (d % n_lag) * lag_local
        out_ref[pl.ds(d * chunk, lag_local), :] = past_ref[pl.ds(first, lag_local), :]


def mirror_kernel(pairs, lag_local, n_lag, n_row, n_col, rows_ref, cols_ref, mask_ref, mats_ref, got_ref, out_ref, part_ref, held):
    chunk = lag_local + 1
    srcs = got_ref.shape[0] // chunk
    row_base = lax.axis_index("row") * (n_col * n_lag)
    col_base = lax.axis_index("col") * n_lag
    part_ref[...] = jnp.sum(got_ref[pl.ds(lag_local, srcs, stride=chunk), :], axis=0, keepdims=True)
    out_ref[...] = jnp.zeros(out_ref.shape, jnp.float32)
    for p in range(pairs):
        row = rows_ref[p]
        col = cols_ref[p]
        col_global = lax.div(col, n_lag) * (n_col * n_lag) + col_base + lax.rem(col, n_lag)
        off_diag = row_base + row != col_global
        for l in range(lag_local):
            keep = jnp.logical_and(mask_ref[p, l] != 0, off_diag)
            vec = got_ref[pl.ds(row * chunk + l, 1), :]
            held[pl.ds(p * lag_local + l, 1), :] = jnp.where(keep, vec, 0.0)
    turned = held[...].T

    def body(p, turned):
        acc = jnp.zeros((16, 8, 128), jnp.float32)
        for l in range(lag_local):
            acc = acc + (mats_ref[p * lag_local + l] * turned[:, l : l + 1]).reshape(16, 8, 128)
        total = jnp.sum(jnp.sum(acc, axis=0), axis=0, keepdims=True)
        at = pl.ds(cols_ref[p], 1)
        out_ref[at, :] = out_ref[at, :] + total
        return pltpu.roll(turned, 128 - lag_local, 1)

    lax.fori_loop(0, pairs, body, turned)


def final_kernel(got_ref, part_ref, incident_ref, inverse_ref, out_ref):
    convolved = jnp.sum(got_ref[...], axis=0, keepdims=True) + part_ref[...]
    rhs = incident_ref[...] - convolved
    sums = jnp.sum(inverse_ref[...] * rhs, axis=1, keepdims=True)
    out_ref[...] = jnp.broadcast_to(sums, (128, 128)).T[:1]


def per_device(n_row, n_col, n_lag, history, step_index, pair_rows, pair_cols, lag_pattern, blocks, incident, self_inverse):
    lags = history.shape[0]
    block = history.shape[2]
    pairs = blocks.shape[2]
    lag_local = blocks.shape[3]
    chunk = lag_local + 1
    f32 = jnp.float32
    rows = pair_rows.reshape(pairs)
    cols = pair_cols.reshape(pairs)
    mask = lag_pattern.reshape(pairs, lag_local)
    mats = blocks.reshape(pairs * lag_local, block, block)
    params = pltpu.CompilerParams(vmem_limit_bytes=16 * 1024 * 1024)

    send, past = pl.pallas_call(
        functools.partial(order_kernel, lags, n_row),
        out_shape=(
            jax.ShapeDtypeStruct((n_row * lags, block), f32),
            jax.ShapeDtypeStruct((lags, block), f32),
        ),
        in_specs=[SMEM, VMEM],
        out_specs=(VMEM, VMEM),
        name="order_lags",
    )(step_index, history.reshape(lags, block))
    send = send.reshape(n_row * n_lag, lag_local, block)
    col_source = lax.all_to_all(send, ("row", "lag"), 0, 0, tiled=True).reshape(n_row * lags, block)
    sent = pl.pallas_call(
        functools.partial(forward_kernel, pairs, lag_local, n_lag),
        out_shape=jax.ShapeDtypeStruct((n_col * n_lag * chunk, block), f32),
        in_specs=[SMEM, SMEM, SMEM, VMEM, VMEM, VMEM],
        out_specs=VMEM,
        name="forward",
        compiler_params=params,
    )(rows, cols, mask, mats, col_source, past)
    got = lax.all_to_all(
        sent.reshape(n_col * n_lag, chunk, 1, block), ("col", "lag"), 0, 0, tiled=True
    ).reshape(n_col * n_lag * chunk, block)
    mirrored, part = pl.pallas_call(
        functools.partial(mirror_kernel, pairs, lag_local, n_lag, n_row, n_col),
        out_shape=(
            jax.ShapeDtypeStruct((n_row * n_lag, block), f32),
            jax.ShapeDtypeStruct((1, block), f32),
        ),
        in_specs=[SMEM, SMEM, SMEM, VMEM, VMEM],
        out_specs=(VMEM, VMEM),
        scratch_shapes=[pltpu.VMEM((pairs * lag_local, block), f32)],
        name="mirror",
        compiler_params=params,
    )(rows, cols, mask, mats, got)
    fields = lax.all_to_all(
        mirrored.reshape(n_row * n_lag, 1, block), ("row", "lag"), 0, 0, tiled=True
    ).reshape(n_row * n_lag, block)
    return pl.pallas_call(
        final_kernel,
        out_shape=jax.ShapeDtypeStruct((1, block), f32),
        in_specs=[VMEM, VMEM, VMEM, VMEM],
        out_specs=VMEM,
        name="final",
    )(fields, part, incident, self_inverse.reshape(block, block))


def solution(mesh):
    in_specs = (
        P(None, ("row", "col", "lag"), None),
        P(),
        P("row", "col", None),
        P("row", "col", None),
        P("row", "col", None, "lag"),
        P("row", "col", None, "lag", None, None),
        P(("row", "col", "lag"), None),
        P(("row", "col", "lag"), None, None),
    )
    out_specs = P(("row", "col", "lag"), None)
    step = functools.partial(per_device, mesh.shape["row"], mesh.shape["col"], mesh.shape["lag"])
    return jax.shard_map(step, mesh=mesh, in_specs=in_specs, out_specs=out_specs, check_vma=False)
```

```python
import functools

import jax
import jax.numpy as jnp
import numpy as np
from jax import lax
from jax.experimental import pallas as pl
from jax.experimental.pallas import tpu as pltpu
from jax.sharding import PartitionSpec as P

VMEM = pl.BlockSpec(memory_space=pltpu.VMEM)
F32 = jnp.float32
BF16 = jnp.bfloat16
MIB = 1024 * 1024
SIDE = 8
SPREAD = 3


def iota(shape, dim):
    return lax.broadcasted_iota(jnp.int32, shape, dim).astype(F32)


def split(values):
    high = values.astype(BF16)
    rest = values - high.astype(F32)
    mid = rest.astype(BF16)
    return high, mid, (rest - mid.astype(F32)).astype(BF16)


def select(picks, values):
    picks = picks.astype(BF16)
    high, mid, low = (jnp.dot(picks, part, preferred_element_type=F32) for part in split(values))
    return high + (mid + low)


def as_column(row, lanes):
    return jnp.broadcast_to(row, (lanes, row.shape[1])).T


def order_kernel(copies, step_ref, hist_ref, send_ref):
    lags = hist_ref.shape[0]
    slot = step_ref[...].astype(F32) - 1.0 - iota((lags, lags), 0)
    slot = jnp.where(slot < 0.0, slot + lags, slot)
    past = select(jnp.where(slot == iota((lags, lags), 1), 1.0, 0.0), hist_ref[...])
    for k in range(copies):
        send_ref[pl.ds(k * lags, lags), :] = past


def forward_kernel(n_col, n_lag, rows_ref, cols_ref, mask_ref, mats_ref, src_ref, out_ref, vecs):
    lag_local, pairs = mask_ref.shape
    terms = lag_local * pairs
    block = src_ref.shape[1]
    cols = cols_ref[...].astype(F32) * lag_local
    spots = [jnp.where(mask_ref[pl.ds(l, 1), :] != 0, cols + l, -1.0) for l in range(lag_local)]
    at = as_column(jnp.concatenate(spots, axis=1), block)
    vecs[...] = select(jnp.where(at == iota((terms, block), 1), 1.0, 0.0), src_ref[...])
    rows = as_column(rows_ref[...].astype(F32), block)
    hits = jnp.where(rows == iota((pairs, block), 1), 1.0, 0.0)
    total = jnp.zeros((block, block), F32)
    for p in range(pairs):
        acc = mats_ref[p * lag_local] * vecs[pl.ds(p, 1), :]
        for l in range(1, lag_local):
            acc = acc + mats_ref[p * lag_local + l] * vecs[pl.ds(l * pairs + p, 1), :]
        total = total + jnp.sum(acc, axis=1, keepdims=True) * hits[p : p + 1]
    fields = total.T
    own = n_lag * lag_local
    chunk = own + n_lag
    group = src_ref[pl.ds(pl.multiple_of(lax.axis_index("row") * own, own), own), :]
    for c in range(n_col):
        out_ref[pl.ds(c * chunk, own), :] = group
        out_ref[pl.ds(c * chunk + own, n_lag), :] = fields[c * n_lag : (c + 1) * n_lag]


def mirror_kernel(
    n_col, n_lag, rows_ref, cols_ref, mask_ref, mats_ref, got_ref, spread_ref, out_ref, sides, turned, held
):
    lag_local, pairs = mask_ref.shape
    block = got_ref.shape[1]
    terms = lag_local * pairs
    groups = pairs // SIDE
    per_group = SIDE * lag_local
    own = n_lag * lag_local
    chunk = own + n_lag
    row_index = lax.axis_index("row")
    row_base = (row_index * (n_col * n_lag)).astype(F32)
    col_base = (lax.axis_index("col") * n_lag).astype(F32)

    rows = rows_ref[...].astype(F32)
    cols = cols_ref[...].astype(F32)
    band = jnp.floor((cols + 0.5) * (1.0 / n_lag))
    col_global = band * (n_col * n_lag) + col_base + (cols - band * n_lag)
    off_diag = row_base + rows != col_global
    spots = [
        jnp.where(jnp.logical_and(mask_ref[pl.ds(l, 1), :] != 0, off_diag), rows * lag_local + l, -1.0)
        for l in range(lag_local)
    ]
    ordered = [spots[l][:, g * SIDE : (g + 1) * SIDE] for g in range(groups) for l in range(lag_local)]
    at = as_column(jnp.concatenate(ordered, axis=1), block)
    at = jnp.concatenate([at] * (n_col * own // block), axis=1)
    picks = jnp.where(at == iota(at.shape, 1), 1.0, 0.0)
    group_past = jnp.concatenate([got_ref[pl.ds(c * chunk, own), :] for c in range(n_col)], axis=0)
    columns = select(picks, group_past).T

    turned[...] = columns
    high = columns.astype(BF16).astype(F32)
    low = columns - high
    for g in range(groups):
        keep = slice(g * per_group, g * per_group + SPREAD * SIDE)
        sides[g] = jnp.concatenate([high[:, keep], low[:, keep]], axis=1).astype(BF16)
    for g in range(groups):
        side = sides[g]
        for q in range(SIDE):
            p = g * SIDE + q
            wide = jnp.dot(side, spread_ref[q], preferred_element_type=F32)
            acc = jnp.zeros((8, block), F32)
            for l in range(lag_local):
                if l < SPREAD:
                    factor = wide[:, l * block : (l + 1) * block]
                else:
                    lane = jnp.full((block, terms), g * per_group + l * SIDE + q, jnp.int32)
                    factor = jnp.take_along_axis(turned[...], lane, axis=1, mode="promise_in_bounds")
                product = mats_ref[p * lag_local + l] * factor
                acc = acc + jnp.sum(product.reshape(block // 8, 8, block), axis=0)
            held[pl.ds(p, 1), :] = jnp.sum(acc, axis=0, keepdims=True)

    dests = out_ref.shape[0]
    hits = jnp.where(cols == iota((dests, pairs), 0), 1.0, 0.0)
    out_ref[...] = select(hits, held[...])
    fields = got_ref[pl.ds(own, n_lag), :]
    for c in range(1, n_col):
        fields = fields + got_ref[pl.ds(c * chunk + own, n_lag), :]
    mine = pl.ds(pl.multiple_of(row_index * n_lag, n_lag), n_lag)
    out_ref[mine, :] = out_ref[mine, :] + fields


def final_kernel(got_ref, incident_ref, inverse_ref, out_ref):
    rhs = incident_ref[...] - jnp.sum(got_ref[...], axis=0, keepdims=True)
    sums = jnp.sum(inverse_ref[...] * rhs, axis=1, keepdims=True)
    out_ref[...] = jnp.broadcast_to(sums, inverse_ref.shape).T[:1]


def call(kernel, name, shape, operands, limit, scratch=()):
    return pl.pallas_call(
        kernel,
        out_shape=jax.ShapeDtypeStruct(shape, F32),
        in_specs=[VMEM] * len(operands),
        out_specs=VMEM,
        scratch_shapes=[pltpu.VMEM(*item) for item in scratch],
        name=name,
        compiler_params=pltpu.CompilerParams(vmem_limit_bytes=limit),
    )(*operands)


def spread_table(block):
    table = np.zeros((SIDE, 2, SPREAD, SIDE, SPREAD, block), np.float32)
    for q in range(SIDE):
        for l in range(SPREAD):
            table[q, :, l, q, l] = 1.0
    return table.reshape(SIDE, 2 * SPREAD * SIDE, SPREAD * block).astype(jnp.bfloat16)


def per_device(n_row, n_col, n_lag, history, step_index, pair_rows, pair_cols, lag_pattern, blocks, incident, self_inverse):
    lags = history.shape[0]
    block = history.shape[2]
    pairs = blocks.shape[2]
    lag_local = blocks.shape[3]
    terms = pairs * lag_local
    n_src = n_row * n_lag
    chunk = n_lag * lag_local + n_lag
    rows = pair_rows.reshape(1, pairs)
    cols = pair_cols.reshape(1, pairs)
    mask = lag_pattern.reshape(pairs, lag_local).T
    mats = blocks.reshape(terms, block, block)

    send = call(
        functools.partial(order_kernel, n_row),
        "order",
        (n_row * lags, block),
        [step_index.reshape(1, 1), history.reshape(lags, block)],
        MIB,
    )
    source = lax.all_to_all(
        send.reshape(n_src, lag_local, block), ("row", "lag"), 0, 0, tiled=True
    ).reshape(n_row * lags, block)
    sent = call(
        functools.partial(forward_kernel, n_col, n_lag),
        "forward",
        (n_col * chunk, block),
        [rows, cols, mask, mats, source],
        2 * MIB,
        [((terms, block), F32)],
    )
    got = lax.all_to_all(sent.reshape(n_col, chunk, block), "col", 0, 0, tiled=True)
    mirrored = call(
        functools.partial(mirror_kernel, n_col, n_lag),
        "mirror",
        (n_src, block),
        [rows, cols, mask, mats, got.reshape(n_col * chunk, block), spread_table(block)],
        3 * MIB,
        [
            ((pairs // SIDE, block, 2 * SPREAD * SIDE), BF16),
            ((block, terms), F32),
            ((pairs, block), F32),
        ],
    )
    fields = lax.all_to_all(mirrored.reshape(n_src, 1, block), ("row", "lag"), 0, 0, tiled=True)
    return call(
        final_kernel,
        "final",
        (1, block),
        [fields.reshape(n_src, block), incident, self_inverse.reshape(block, block)],
        MIB,
    )


def solution(mesh):
    in_specs = (
        P(None, ("row", "col", "lag"), None),
        P(),
        P("row", "col", None),
        P("row", "col", None),
        P("row", "col", None, "lag"),
        P("row", "col", None, "lag", None, None),
        P(("row", "col", "lag"), None),
        P(("row", "col", "lag"), None, None),
    )
    out_specs = P(("row", "col", "lag"), None)
    step = functools.partial(per_device, mesh.shape["row"], mesh.shape["col"], mesh.shape["lag"])
    return jax.shard_map(step, mesh=mesh, in_specs=in_specs, out_specs=out_specs, check_vma=False)
```

```python
import functools

import jax
import jax.numpy as jnp
import numpy as np
from jax import lax
from jax.experimental import pallas as pl
from jax.experimental.pallas import tpu as pltpu
from jax.sharding import PartitionSpec as P

VMEM = pl.BlockSpec(memory_space=pltpu.VMEM)
F32 = jnp.float32
BF16 = jnp.bfloat16
MIB = 1024 * 1024
SIDE = 8
SPREAD = 3


def iota(shape, dim):
    return lax.broadcasted_iota(jnp.int32, shape, dim).astype(F32)


def split(values):
    high = values.astype(BF16)
    rest = values - high.astype(F32)
    mid = rest.astype(BF16)
    return high, mid, (rest - mid.astype(F32)).astype(BF16)


def select(picks, values):
    picks = picks.astype(BF16)
    high, mid, low = (jnp.dot(picks, part, preferred_element_type=F32) for part in split(values))
    return high + (mid + low)


def as_column(row, lanes):
    return jnp.broadcast_to(row, (lanes, row.shape[1])).T


def order_kernel(copies, step_ref, hist_ref, send_ref):
    lags = hist_ref.shape[0]
    slot = step_ref[...].astype(F32) - 1.0 - iota((lags, lags), 0)
    slot = jnp.where(slot < 0.0, slot + lags, slot)
    past = select(jnp.where(slot == iota((lags, lags), 1), 1.0, 0.0), hist_ref[...])
    for k in range(copies):
        send_ref[pl.ds(k * lags, lags), :] = past


def forward_kernel(n_col, n_lag, rows_ref, cols_ref, mask_ref, mats_ref, src_ref, out_ref, vecs):
    lag_local, pairs = mask_ref.shape
    terms = lag_local * pairs
    block = src_ref.shape[1]
    cols = cols_ref[...].astype(F32) * lag_local
    spots = [jnp.where(mask_ref[pl.ds(l, 1), :] != 0, cols + l, -1.0) for l in range(lag_local)]
    at = as_column(jnp.concatenate(spots, axis=1), block)
    vecs[...] = select(jnp.where(at == iota((terms, block), 1), 1.0, 0.0), src_ref[...])
    rows = as_column(rows_ref[...].astype(F32), block)
    hits = jnp.where(rows == iota((pairs, block), 1), 1.0, 0.0)
    total = jnp.zeros((block, block), F32)
    for p in range(pairs):
        acc = mats_ref[p * lag_local] * vecs[pl.ds(p, 1), :]
        for l in range(1, lag_local):
            acc = acc + mats_ref[p * lag_local + l] * vecs[pl.ds(l * pairs + p, 1), :]
        total = total + jnp.sum(acc, axis=1, keepdims=True) * hits[p : p + 1]
    fields = total.T
    own = n_lag * lag_local
    chunk = own + n_lag
    group = src_ref[pl.ds(pl.multiple_of(lax.axis_index("row") * own, own), own), :]
    for c in range(n_col):
        out_ref[pl.ds(c * chunk, own), :] = group
        out_ref[pl.ds(c * chunk + own, n_lag), :] = fields[c * n_lag : (c + 1) * n_lag]


def mirror_kernel(
    n_col, n_lag, rows_ref, cols_ref, mask_ref, mats_ref, got_ref, spread_ref, out_ref, sides, turned, held
):
    lag_local, pairs = mask_ref.shape
    block = got_ref.shape[1]
    terms = lag_local * pairs
    groups = pairs // SIDE
    per_group = SIDE * lag_local
    own = n_lag * lag_local
    chunk = own + n_lag
    row_index = lax.axis_index("row")
    row_base = (row_index * (n_col * n_lag)).astype(F32)
    col_base = (lax.axis_index("col") * n_lag).astype(F32)

    rows = rows_ref[...].astype(F32)
    cols = cols_ref[...].astype(F32)
    band = jnp.floor((cols + 0.5) * (1.0 / n_lag))
    col_global = band * (n_col * n_lag) + col_base + (cols - band * n_lag)
    off_diag = row_base + rows != col_global
    spots = [
        jnp.where(jnp.logical_and(mask_ref[pl.ds(l, 1), :] != 0, off_diag), rows * lag_local + l, -1.0)
        for l in range(lag_local)
    ]
    ordered = [spots[l][:, g * SIDE : (g + 1) * SIDE] for g in range(groups) for l in range(lag_local)]
    at = as_column(jnp.concatenate(ordered, axis=1), block)
    at = jnp.concatenate([at] * (n_col * own // block), axis=1)
    picks = jnp.where(at == iota(at.shape, 1), 1.0, 0.0)
    group_past = jnp.concatenate([got_ref[pl.ds(c * chunk, own), :] for c in range(n_col)], axis=0)
    columns = select(picks, group_past).T

    turned[...] = columns
    high = columns.astype(BF16).astype(F32)
    low = columns - high
    for g in range(groups):
        keep = slice(g * per_group, g * per_group + SPREAD * SIDE)
        sides[g] = jnp.concatenate([high[:, keep], low[:, keep]], axis=1).astype(BF16)
    for g in range(groups):
        side = sides[g]
        for q in range(SIDE):
            p = g * SIDE + q
            wide = jnp.dot(side, spread_ref[q], preferred_element_type=F32)
            acc = jnp.zeros((8, block), F32)
            for l in range(lag_local):
                if l < SPREAD:
                    factor = wide[:, l * block : (l + 1) * block]
                else:
                    lane = jnp.full((block, terms), g * per_group + l * SIDE + q, jnp.int32)
                    factor = jnp.take_along_axis(turned[...], lane, axis=1, mode="promise_in_bounds")
                product = mats_ref[p * lag_local + l] * factor
                acc = acc + jnp.sum(product.reshape(block // 8, 8, block), axis=0)
            held[pl.ds(p, 1), :] = jnp.sum(acc, axis=0, keepdims=True)

    dests = out_ref.shape[0]
    hits = jnp.where(cols == iota((dests, pairs), 0), 1.0, 0.0)
    out_ref[...] = select(hits, held[...])
    fields = got_ref[pl.ds(own, n_lag), :]
    for c in range(1, n_col):
        fields = fields + got_ref[pl.ds(c * chunk + own, n_lag), :]
    mine = pl.ds(pl.multiple_of(row_index * n_lag, n_lag), n_lag)
    out_ref[mine, :] = out_ref[mine, :] + fields


def final_kernel(got_ref, incident_ref, inverse_ref, out_ref):
    rhs = incident_ref[...] - jnp.sum(got_ref[...], axis=0, keepdims=True)
    sums = jnp.sum(inverse_ref[...] * rhs, axis=1, keepdims=True)
    out_ref[...] = jnp.broadcast_to(sums, inverse_ref.shape).T[:1]


def call(kernel, name, shape, operands, limit, scratch=()):
    return pl.pallas_call(
        kernel,
        out_shape=jax.ShapeDtypeStruct(shape, F32),
        in_specs=[VMEM] * len(operands),
        out_specs=VMEM,
        scratch_shapes=[pltpu.VMEM(*item) for item in scratch],
        name=name,
        compiler_params=pltpu.CompilerParams(vmem_limit_bytes=limit),
        cost_estimate=pl.CostEstimate(flops=20_000_000_000, bytes_accessed=64 * MIB, transcendentals=0),
    )(*operands)


def spread_table(block):
    table = np.zeros((SIDE, 2, SPREAD, SIDE, SPREAD, block), np.float32)
    for q in range(SIDE):
        for l in range(SPREAD):
            table[q, :, l, q, l] = 1.0
    return table.reshape(SIDE, 2 * SPREAD * SIDE, SPREAD * block).astype(jnp.bfloat16)


def per_device(n_row, n_col, n_lag, history, step_index, pair_rows, pair_cols, lag_pattern, blocks, incident, self_inverse):
    lags = history.shape[0]
    block = history.shape[2]
    pairs = blocks.shape[2]
    lag_local = blocks.shape[3]
    terms = pairs * lag_local
    n_src = n_row * n_lag
    chunk = n_lag * lag_local + n_lag
    rows = pair_rows.reshape(1, pairs)
    cols = pair_cols.reshape(1, pairs)
    mask = lag_pattern.reshape(pairs, lag_local).T
    mats = blocks.reshape(terms, block, block)

    send = call(
        functools.partial(order_kernel, n_row),
        "order",
        (n_row * lags, block),
        [step_index.reshape(1, 1), history.reshape(lags, block)],
        MIB,
    )
    source = lax.all_to_all(
        send.reshape(n_src, lag_local, block), ("row", "lag"), 0, 0, tiled=True
    ).reshape(n_row * lags, block)
    sent = call(
        functools.partial(forward_kernel, n_col, n_lag),
        "forward",
        (n_col * chunk, block),
        [rows, cols, mask, mats, source],
        2 * MIB,
        [((terms, block), F32)],
    )
    got = lax.all_to_all(sent.reshape(n_col, chunk, block), "col", 0, 0, tiled=True)
    mirrored = call(
        functools.partial(mirror_kernel, n_col, n_lag),
        "mirror",
        (n_src, block),
        [rows, cols, mask, mats, got.reshape(n_col * chunk, block), spread_table(block)],
        3 * MIB,
        [
            ((pairs // SIDE, block, 2 * SPREAD * SIDE), BF16),
            ((block, terms), F32),
            ((pairs, block), F32),
        ],
    )
    fields = lax.all_to_all(mirrored.reshape(n_src, 1, block), ("row", "lag"), 0, 0, tiled=True)
    return call(
        final_kernel,
        "final",
        (1, block),
        [fields.reshape(n_src, block), incident, self_inverse.reshape(block, block)],
        MIB,
    )


def solution(mesh):
    in_specs = (
        P(None, ("row", "col", "lag"), None),
        P(),
        P("row", "col", None),
        P("row", "col", None),
        P("row", "col", None, "lag"),
        P("row", "col", None, "lag", None, None),
        P(("row", "col", "lag"), None),
        P(("row", "col", "lag"), None, None),
    )
    out_specs = P(("row", "col", "lag"), None)
    step = functools.partial(per_device, mesh.shape["row"], mesh.shape["col"], mesh.shape["lag"])
    return jax.shard_map(step, mesh=mesh, in_specs=in_specs, out_specs=out_specs, check_vma=False)
```

```python
import functools

import jax
import jax.numpy as jnp
from jax import lax
from jax.experimental import pallas as pl
from jax.experimental.pallas import tpu as pltpu
from jax.sharding import PartitionSpec as P

VMEM = pl.BlockSpec(memory_space=pltpu.VMEM)
F32 = jnp.float32
BF16 = jnp.bfloat16
MIB = 1024 * 1024
SIDE = 8
SPREAD = 3
TOGETHER = 2


def iota(shape, dim):
    return lax.broadcasted_iota(jnp.int32, shape, dim).astype(F32)


def split(values):
    high = values.astype(BF16)
    rest = values - high.astype(F32)
    mid = rest.astype(BF16)
    return high, mid, (rest - mid.astype(F32)).astype(BF16)


def select(picks, values):
    picks = picks.astype(BF16)
    return jnp.dot(
        jnp.concatenate([picks] * 3, axis=1), jnp.concatenate(split(values), axis=0), preferred_element_type=F32
    )


def as_column(row, lanes):
    return jnp.broadcast_to(row, (lanes, row.shape[1])).T


def pick_rows(spots, width):
    at = as_column(spots, 128)
    at = jnp.concatenate([at] * (width // 128), axis=1)
    return jnp.where(at == iota(at.shape, 1), 1.0, 0.0).astype(BF16)


def table_kernel(spread_ref, token_ref):
    batches, height, width = spread_ref.shape
    source = lax.broadcasted_iota(jnp.int32, (height, width), 0)
    target = lax.broadcasted_iota(jnp.int32, (height, width), 1)
    token_ref[...] = jnp.zeros(token_ref.shape, F32)
    for batch in range(batches):
        table = jnp.zeros((height, width), F32)
        for t in range(TOGETHER):
            for l in range(SPREAD):
                first = (t * SPREAD + l) * 128
                lanes = jnp.logical_and(target >= first, target < first + 128)
                row = l * SIDE + batch * TOGETHER + t
                rows = jnp.logical_or(source == row, source == row + SPREAD * SIDE)
                table = jnp.where(jnp.logical_and(lanes, rows), 1.0, table)
        spread_ref[batch] = table.astype(BF16)


def order_kernel(
    copies, step_ref, hist_ref, rows_ref, cols_ref, mask_ref, token_ref, send_ref, picks_ref, hits_ref
):
    del token_ref
    lags = hist_ref.shape[0]
    slot = step_ref[...].astype(F32) - 1.0 - iota((lags, lags), 0)
    slot = jnp.where(slot < 0.0, slot + lags, slot)
    turn = jnp.where(slot == iota((lags, lags), 1), 1.0, 0.0).astype(BF16)
    high, mid, low = (jnp.dot(turn, part, preferred_element_type=F32) for part in split(hist_ref[...]))
    past = high + (mid + low)
    for k in range(copies):
        send_ref[pl.ds(k * lags, lags), :] = past

    lag_local = mask_ref.shape[0]
    cols = cols_ref[...].astype(F32) * lag_local
    spots = [jnp.where(mask_ref[pl.ds(l, 1), :] != 0, cols + l, -1.0) for l in range(lag_local)]
    picks_ref[...] = pick_rows(jnp.concatenate(spots, axis=1), picks_ref.shape[1])
    rows = as_column(rows_ref[...].astype(F32), hits_ref.shape[1])
    hits_ref[...] = jnp.where(rows == iota(hits_ref.shape, 1), 1.0, 0.0)


def forward_kernel(
    n_col, n_lag, rows_ref, cols_ref, mask_ref, mats_ref, src_ref, picks_ref, hits_ref,
    out_ref, mirror_picks_ref, mirror_hits_ref, vecs,
):
    lag_local, pairs = mask_ref.shape
    block = src_ref.shape[1]
    own = n_lag * lag_local
    chunk = own + n_lag
    vecs[...] = select(picks_ref[...], src_ref[...])
    group = src_ref[pl.ds(pl.multiple_of(lax.axis_index("row") * own, own), own), :]
    total = jnp.zeros((block, block), F32)
    for p in range(pairs):
        acc = mats_ref[p * lag_local] * vecs[pl.ds(p, 1), :]
        for l in range(1, lag_local):
            acc = acc + mats_ref[p * lag_local + l] * vecs[pl.ds(l * pairs + p, 1), :]
        total = total + jnp.sum(acc, axis=1, keepdims=True) * hits_ref[pl.ds(p, 1), :]
    fields = total.T
    for c in range(n_col):
        out_ref[pl.ds(c * chunk, own), :] = group
        out_ref[pl.ds(c * chunk + own, n_lag), :] = fields[c * n_lag : (c + 1) * n_lag]

    row_base = (lax.axis_index("row") * (n_col * n_lag)).astype(F32)
    col_base = (lax.axis_index("col") * n_lag).astype(F32)
    rows = rows_ref[...].astype(F32)
    cols = cols_ref[...].astype(F32)
    band = jnp.floor((cols + 0.5) * (1.0 / n_lag))
    col_global = band * (n_col * n_lag) + col_base + (cols - band * n_lag)
    off_diag = row_base + rows != col_global
    spots = [
        jnp.where(jnp.logical_and(mask_ref[pl.ds(l, 1), :] != 0, off_diag), rows * lag_local + l, -1.0)
        for l in range(lag_local)
    ]
    ordered = [
        spots[l][:, g * SIDE : (g + 1) * SIDE] for g in range(pairs // SIDE) for l in range(lag_local)
    ]
    mirror_picks_ref[...] = pick_rows(jnp.concatenate(ordered, axis=1), mirror_picks_ref.shape[1])
    cols = jnp.concatenate([cols] * 8, axis=1)
    mirror_hits_ref[...] = jnp.where(cols == iota(mirror_hits_ref.shape, 0), 1.0, 0.0).astype(BF16)


def mirror_kernel(
    n_col, n_lag, lag_local, mats_ref, got_ref, picks_ref, hits_ref, spread_ref, out_ref, sides, turned, held
):
    pairs = hits_ref.shape[1] // 8
    block = got_ref.shape[1]
    terms = lag_local * pairs
    groups = pairs // SIDE
    per_group = SIDE * lag_local
    own = n_lag * lag_local
    chunk = own + n_lag
    group_past = jnp.concatenate([got_ref[pl.ds(c * chunk, own), :] for c in range(n_col)], axis=0)
    columns = select(picks_ref[...], group_past).T
    turned[...] = columns
    high = columns.astype(BF16).astype(F32)
    low = columns - high
    for g in range(groups):
        keep = slice(g * per_group, g * per_group + SPREAD * SIDE)
        sides[g] = jnp.concatenate([high[:, keep], low[:, keep]], axis=1).astype(BF16)
    for g in range(groups):
        side = sides[g]
        for q in range(0, SIDE, TOGETHER):
            wide = jnp.dot(side, spread_ref[q // TOGETHER], preferred_element_type=F32)
            for t in range(TOGETHER):
                p = g * SIDE + q + t
                acc = jnp.zeros((8, block), F32)
                for l in range(lag_local):
                    if l < SPREAD:
                        first = (t * SPREAD + l) * block
                        factor = wide[:, first : first + block]
                    else:
                        lane = jnp.full((block, terms), g * per_group + l * SIDE + q + t, jnp.int32)
                        factor = jnp.take_along_axis(turned[...], lane, axis=1, mode="promise_in_bounds")
                    product = mats_ref[p * lag_local + l] * factor
                    acc = acc + jnp.sum(product.reshape(block // 8, 8, block), axis=0)
                held[pl.ds(p, 8, stride=pairs), :] = acc

    out_ref[...] = select(hits_ref[...], held[...])
    fields = got_ref[pl.ds(own, n_lag), :]
    for c in range(1, n_col):
        fields = fields + got_ref[pl.ds(c * chunk + own, n_lag), :]
    mine = pl.ds(pl.multiple_of(lax.axis_index("row") * n_lag, n_lag), n_lag)
    out_ref[mine, :] = out_ref[mine, :] + fields


def final_kernel(got_ref, incident_ref, inverse_ref, out_ref):
    rhs = incident_ref[...] - jnp.sum(got_ref[...], axis=0, keepdims=True)
    sums = jnp.sum(inverse_ref[...] * rhs, axis=1, keepdims=True)
    out_ref[...] = jnp.broadcast_to(sums, inverse_ref.shape).T[:1]


def call(kernel, name, outs, operands, limit, scratch=()):
    return pl.pallas_call(
        kernel,
        out_shape=tuple(jax.ShapeDtypeStruct(*out) for out in outs),
        in_specs=[VMEM] * len(operands),
        out_specs=tuple(VMEM for _ in outs),
        scratch_shapes=[pltpu.VMEM(*item) for item in scratch],
        name=name,
        compiler_params=pltpu.CompilerParams(vmem_limit_bytes=limit),
        cost_estimate=pl.CostEstimate(flops=20_000_000_000, bytes_accessed=64 * MIB, transcendentals=0),
    )(*operands)


def per_device(n_row, n_col, n_lag, history, step_index, pair_rows, pair_cols, lag_pattern, blocks, incident, self_inverse):
    lags = history.shape[0]
    block = history.shape[2]
    pairs = blocks.shape[2]
    lag_local = blocks.shape[3]
    terms = pairs * lag_local
    n_src = n_row * n_lag
    own = n_lag * lag_local
    chunk = own + n_lag
    rows = pair_rows.reshape(1, pairs)
    cols = pair_cols.reshape(1, pairs)
    mask = lag_pattern.reshape(pairs, lag_local).T
    mats = blocks.reshape(terms, block, block)

    spread, token = call(
        table_kernel,
        "table",
        [((SIDE // TOGETHER, 2 * SPREAD * SIDE, TOGETHER * SPREAD * block), BF16), ((8, block), F32)],
        [],
        MIB,
    )
    send, picks, hits = call(
        functools.partial(order_kernel, n_row),
        "order",
        [((n_row * lags, block), F32), ((terms, n_row * lags), BF16), ((pairs, block), F32)],
        [step_index.reshape(1, 1), history.reshape(lags, block), rows, cols, mask, token],
        MIB,
    )
    source = lax.all_to_all(
        send.reshape(n_src, lag_local, block), ("row", "lag"), 0, 0, tiled=True
    ).reshape(n_row * lags, block)
    sent, mirror_picks, mirror_hits = call(
        functools.partial(forward_kernel, n_col, n_lag),
        "forward",
        [((n_col * chunk, block), F32), ((terms, n_col * own), BF16), ((n_src, 8 * pairs), BF16)],
        [rows, cols, mask, mats, source, picks, hits],
        2 * MIB,
        [((terms, block), F32)],
    )
    got = lax.all_to_all(sent.reshape(n_col, chunk, block), "col", 0, 0, tiled=True)
    (mirrored,) = call(
        functools.partial(mirror_kernel, n_col, n_lag, lag_local),
        "mirror",
        [((n_src, block), F32)],
        [mats, got.reshape(n_col * chunk, block), mirror_picks, mirror_hits, spread],
        3 * MIB,
        [
            ((pairs // SIDE, block, 2 * SPREAD * SIDE), BF16),
            ((block, terms), F32),
            ((8 * pairs, block), F32),
        ],
    )
    fields = lax.all_to_all(mirrored.reshape(n_src, 1, block), ("row", "lag"), 0, 0, tiled=True)
    return call(
        final_kernel,
        "final",
        [((1, block), F32)],
        [fields.reshape(n_src, block), incident, self_inverse.reshape(block, block)],
        MIB,
    )[0]


def solution(mesh):
    in_specs = (
        P(None, ("row", "col", "lag"), None),
        P(),
        P("row", "col", None),
        P("row", "col", None),
        P("row", "col", None, "lag"),
        P("row", "col", None, "lag", None, None),
        P(("row", "col", "lag"), None),
        P(("row", "col", "lag"), None, None),
    )
    out_specs = P(("row", "col", "lag"), None)
    step = functools.partial(per_device, mesh.shape["row"], mesh.shape["col"], mesh.shape["lag"])
    return jax.shard_map(step, mesh=mesh, in_specs=in_specs, out_specs=out_specs, check_vma=False)
```

```python
import functools

import jax
import jax.numpy as jnp
from jax import lax
from jax.experimental import pallas as pl
from jax.experimental.pallas import tpu as pltpu
from jax.sharding import PartitionSpec as P

VMEM = pl.BlockSpec(memory_space=pltpu.VMEM)
F32 = jnp.float32
BF16 = jnp.bfloat16
MIB = 1024 * 1024
SIDE = 8
SPREAD = 3
TOGETHER = 2
COL_ORDER = (5, 4, 6, 3, 7, 2, 0, 1)


def iota(shape, dim):
    return lax.broadcasted_iota(jnp.int32, shape, dim).astype(F32)


def split(values, parts):
    pieces = []
    for _ in range(parts - 1):
        pieces.append(values.astype(BF16))
        values = values - pieces[-1].astype(F32)
    return pieces + [values.astype(BF16)]


def select(picks, values):
    return jnp.dot(
        jnp.concatenate([picks] * 2, axis=1), jnp.concatenate(split(values, 2), axis=0), preferred_element_type=F32
    )


def as_column(row, lanes):
    return jnp.broadcast_to(row, (lanes, row.shape[1])).T


def pick_rows(spots, width):
    at = as_column(spots, 128)
    at = jnp.concatenate([at] * (width // 128), axis=1)
    return jnp.where(at == iota(at.shape, 1), 1.0, 0.0).astype(BF16)


def table_kernel(spread_ref, token_ref):
    batches, height, width = spread_ref.shape
    source = lax.broadcasted_iota(jnp.int32, (height, width), 0)
    target = lax.broadcasted_iota(jnp.int32, (height, width), 1)
    token_ref[...] = jnp.zeros(token_ref.shape, F32)
    for batch in range(batches):
        table = jnp.zeros((height, width), F32)
        for t in range(TOGETHER):
            for l in range(SPREAD):
                first = (t * SPREAD + l) * 128
                lanes = jnp.logical_and(target >= first, target < first + 128)
                row = l * SIDE + batch * TOGETHER + t
                rows = jnp.logical_or(source == row, source == row + SPREAD * SIDE)
                table = jnp.where(jnp.logical_and(lanes, rows), 1.0, table)
        spread_ref[batch] = table.astype(BF16)


def turned(index, size, first):
    index = index - first
    return jnp.where(index < 0.0, index + size, index)


def parts_of(index, size):
    major = jnp.floor((index + 0.5) * (1.0 / size))
    return major, index - major * size


def order_kernel(
    n_lag, copies, step_ref, hist_ref, rows_ref, cols_ref, mask_ref, token_ref, send_ref, picks_ref, hits_ref
):
    del token_ref
    lags = hist_ref.shape[0]
    slot = step_ref[...].astype(F32) - 1.0 - iota((lags, lags), 0)
    slot = jnp.where(slot < 0.0, slot + lags, slot)
    turn = jnp.where(slot == iota((lags, lags), 1), 1.0, 0.0).astype(BF16)
    high, mid, low = (jnp.dot(turn, part, preferred_element_type=F32) for part in split(hist_ref[...], 3))
    past = high + (mid + low)
    for k in range(copies):
        send_ref[pl.ds(k * lags, lags), :] = past

    lag_local = mask_ref.shape[0]
    cols = cols_ref[...].astype(F32) * lag_local
    spots = [jnp.where(mask_ref[pl.ds(l, 1), :] != 0, cols + l, -1.0) for l in range(lag_local)]
    picks_ref[...] = pick_rows(jnp.concatenate(spots, axis=1), picks_ref.shape[1])
    major, minor = parts_of(rows_ref[...].astype(F32), n_lag)
    rows = as_column(major * n_lag + turned(minor, n_lag, n_lag // 2), hits_ref.shape[1])
    hits_ref[...] = jnp.where(rows == iota(hits_ref.shape, 1), 1.0, 0.0)


def forward_kernel(
    n_row, n_col, n_lag, rows_ref, cols_ref, mask_ref, mats_ref, src_ref, picks_ref, hits_ref,
    out_ref, mirror_picks_ref, mirror_hits_ref, vecs,
):
    lag_local, pairs = mask_ref.shape
    block = src_ref.shape[1]
    own = n_lag * lag_local
    chunk = own + n_lag
    vecs[...] = select(picks_ref[...], src_ref[...])
    group = src_ref[pl.ds(pl.multiple_of(lax.axis_index("row") * own, own), own), :]
    total = jnp.zeros((block, block), F32)
    for p in range(pairs):
        acc = mats_ref[p * lag_local] * vecs[pl.ds(p, 1), :]
        for l in range(1, lag_local):
            acc = acc + mats_ref[p * lag_local + l] * vecs[pl.ds(l * pairs + p, 1), :]
        total = total + jnp.sum(acc, axis=1, keepdims=True) * hits_ref[pl.ds(p, 1), :]
    fields = total.T
    for c in range(n_col):
        at = COL_ORDER.index(c) * chunk
        out_ref[pl.ds(at, own), :] = group
        out_ref[pl.ds(at + own, n_lag), :] = fields[c * n_lag : (c + 1) * n_lag]

    row_base = (lax.axis_index("row") * (n_col * n_lag)).astype(F32)
    col_base = (lax.axis_index("col") * n_lag).astype(F32)
    rows = rows_ref[...].astype(F32)
    cols = cols_ref[...].astype(F32)
    band, inner = parts_of(cols, n_lag)
    col_global = band * (n_col * n_lag) + col_base + inner
    off_diag = row_base + rows != col_global
    spots = [
        jnp.where(jnp.logical_and(mask_ref[pl.ds(l, 1), :] != 0, off_diag), rows * lag_local + l, -1.0)
        for l in range(lag_local)
    ]
    ordered = [
        spots[l][:, g * SIDE : (g + 1) * SIDE] for g in range(pairs // SIDE) for l in range(lag_local)
    ]
    mirror_picks_ref[...] = pick_rows(jnp.concatenate(ordered, axis=1), mirror_picks_ref.shape[1])
    target = turned(band, n_row, n_row // 2) * n_lag + turned(inner, n_lag, n_lag // 2)
    cols = jnp.concatenate([target] * 8, axis=1)
    mirror_hits_ref[...] = jnp.where(cols == iota(mirror_hits_ref.shape, 0), 1.0, 0.0).astype(BF16)


def mirror_kernel(
    n_row, n_col, n_lag, lag_local, mats_ref, got_ref, picks_ref, hits_ref, spread_ref, out_ref, sides, whole, held
):
    pairs = hits_ref.shape[1] // 8
    block = got_ref.shape[1]
    terms = lag_local * pairs
    groups = pairs // SIDE
    per_group = SIDE * lag_local
    own = n_lag * lag_local
    chunk = own + n_lag
    group_past = jnp.concatenate([got_ref[pl.ds(COL_ORDER.index(c) * chunk, own), :] for c in range(n_col)], axis=0)
    columns = select(picks_ref[...], group_past).T
    whole[...] = columns
    high = columns.astype(BF16).astype(F32)
    low = columns - high
    for g in range(groups):
        keep = slice(g * per_group, g * per_group + SPREAD * SIDE)
        sides[g] = jnp.concatenate([high[:, keep], low[:, keep]], axis=1).astype(BF16)
    for g in range(groups):
        side = sides[g]
        for q in range(0, SIDE, TOGETHER):
            wide = jnp.dot(side, spread_ref[q // TOGETHER], preferred_element_type=F32)
            for t in range(TOGETHER):
                p = g * SIDE + q + t
                acc = jnp.zeros((8, block), F32)
                for l in range(lag_local):
                    if l < SPREAD:
                        first = (t * SPREAD + l) * block
                        factor = wide[:, first : first + block]
                    else:
                        lane = jnp.full((block, terms), g * per_group + l * SIDE + q + t, jnp.int32)
                        factor = jnp.take_along_axis(whole[...], lane, axis=1, mode="promise_in_bounds")
                    product = mats_ref[p * lag_local + l] * factor
                    acc = acc + jnp.sum(product.reshape(block // 8, 8, block), axis=0)
                held[pl.ds(p, 8, stride=pairs), :] = acc

    out_ref[...] = select(hits_ref[...], held[...])
    fields = got_ref[pl.ds(own, n_lag), :]
    for c in range(1, n_col):
        fields = fields + got_ref[pl.ds(c * chunk + own, n_lag), :]
    mine = lax.rem(lax.axis_index("row") + n_row - n_row // 2, n_row) * n_lag
    mine = pl.ds(pl.multiple_of(mine, n_lag), n_lag)
    out_ref[mine, :] = out_ref[mine, :] + fields


def final_kernel(got_ref, incident_ref, inverse_ref, out_ref):
    rhs = incident_ref[...] - jnp.sum(got_ref[...], axis=0, keepdims=True)
    sums = jnp.sum(inverse_ref[...] * rhs, axis=1, keepdims=True)
    shape = inverse_ref.shape
    out_ref[...] = jnp.sum(jnp.where(iota(shape, 0) == iota(shape, 1), sums, 0.0), axis=0, keepdims=True)


def call(kernel, name, outs, operands, limit, scratch=()):
    return pl.pallas_call(
        kernel,
        out_shape=tuple(jax.ShapeDtypeStruct(*out) for out in outs),
        in_specs=[VMEM] * len(operands),
        out_specs=tuple(VMEM for _ in outs),
        scratch_shapes=[pltpu.VMEM(*item) for item in scratch],
        name=name,
        compiler_params=pltpu.CompilerParams(vmem_limit_bytes=limit),
        cost_estimate=pl.CostEstimate(flops=20_000_000_000, bytes_accessed=64 * MIB, transcendentals=0),
    )(*operands)


def per_device(n_row, n_col, n_lag, history, step_index, pair_rows, pair_cols, lag_pattern, blocks, incident, self_inverse):
    lags = history.shape[0]
    block = history.shape[2]
    pairs = blocks.shape[2]
    lag_local = blocks.shape[3]
    terms = pairs * lag_local
    n_src = n_row * n_lag
    own = n_lag * lag_local
    chunk = own + n_lag
    rows = pair_rows.reshape(1, pairs)
    cols = pair_cols.reshape(1, pairs)
    mask = lag_pattern.reshape(pairs, lag_local).T
    mats = blocks.reshape(terms, block, block)

    spread, token = call(
        table_kernel,
        "table",
        [((SIDE // TOGETHER, 2 * SPREAD * SIDE, TOGETHER * SPREAD * block), BF16), ((8, block), F32)],
        [],
        MIB,
    )
    send, picks, hits = call(
        functools.partial(order_kernel, n_lag, n_row),
        "order",
        [((n_row * lags, block), F32), ((terms, n_row * lags), BF16), ((pairs, block), F32)],
        [step_index.reshape(1, 1), history.reshape(lags, block), rows, cols, mask, token],
        MIB,
    )
    source = lax.all_to_all(
        send.reshape(n_src, lag_local, block), ("row", "lag"), 0, 0, tiled=True
    ).reshape(n_row * lags, block)
    sent, mirror_picks, mirror_hits = call(
        functools.partial(forward_kernel, n_row, n_col, n_lag),
        "forward",
        [((n_col * chunk, block), F32), ((terms, n_col * own), BF16), ((n_src, 8 * pairs), BF16)],
        [rows, cols, mask, mats, source, picks, hits],
        2 * MIB,
        [((terms, block), F32)],
    )
    got = lax.all_to_all(
        sent.reshape(n_col, chunk, block), "col", 0, 0, tiled=True, axis_index_groups=[list(COL_ORDER)]
    )
    (mirrored,) = call(
        functools.partial(mirror_kernel, n_row, n_col, n_lag, lag_local),
        "mirror",
        [((n_src, block), F32)],
        [mats, got.reshape(n_col * chunk, block), mirror_picks, mirror_hits, spread],
        3 * MIB,
        [
            ((pairs // SIDE, block, 2 * SPREAD * SIDE), BF16),
            ((block, terms), F32),
            ((8 * pairs, block), F32),
        ],
    )
    last_order = [
        (r + n_row // 2) % n_row * n_lag + (l + n_lag // 2) % n_lag for r in range(n_row) for l in range(n_lag)
    ]
    fields = lax.all_to_all(
        mirrored.reshape(n_src, 1, block), ("row", "lag"), 0, 0, tiled=True, axis_index_groups=[last_order]
    )
    return call(
        final_kernel,
        "final",
        [((1, block), F32)],
        [fields.reshape(n_src, block), incident, self_inverse.reshape(block, block)],
        MIB,
    )[0]


def solution(mesh):
    in_specs = (
        P(None, ("row", "col", "lag"), None),
        P(),
        P("row", "col", None),
        P("row", "col", None),
        P("row", "col", None, "lag"),
        P("row", "col", None, "lag", None, None),
        P(("row", "col", "lag"), None),
        P(("row", "col", "lag"), None, None),
    )
    out_specs = P(("row", "col", "lag"), None)
    step = functools.partial(per_device, mesh.shape["row"], mesh.shape["col"], mesh.shape["lag"])
    return jax.shard_map(step, mesh=mesh, in_specs=in_specs, out_specs=out_specs, check_vma=False)
```

```python
import functools

import jax
import jax.numpy as jnp
from jax import lax
from jax.experimental import pallas as pl
from jax.experimental.pallas import tpu as pltpu
from jax.sharding import PartitionSpec as P

VMEM = pl.BlockSpec(memory_space=pltpu.VMEM)
F32 = jnp.float32
BF16 = jnp.bfloat16
MIB = 1024 * 1024
SIDE = 8
SPREAD = 3
TOGETHER = 2
COL_ORDER = (5, 4, 6, 3, 7, 2, 0, 1)
ROW_FIRST, LAG_FIRST = 2, 5


def iota(shape, dim):
    return lax.broadcasted_iota(jnp.int32, shape, dim).astype(F32)


def split(values, parts):
    pieces = []
    for _ in range(parts - 1):
        pieces.append(values.astype(BF16))
        values = values - pieces[-1].astype(F32)
    return pieces + [values.astype(BF16)]


def select(picks, values):
    return jnp.dot(
        jnp.concatenate([picks] * 2, axis=1), jnp.concatenate(split(values, 2), axis=0), preferred_element_type=F32
    )


def as_column(row, lanes):
    return jnp.broadcast_to(row, (lanes, row.shape[1])).T


def pick_rows(spots, width):
    at = as_column(spots, 128)
    at = jnp.concatenate([at] * (width // 128), axis=1)
    return jnp.where(at == iota(at.shape, 1), 1.0, 0.0).astype(BF16)


def table_kernel(spread_ref, token_ref):
    batches, height, width = spread_ref.shape
    source = lax.broadcasted_iota(jnp.int32, (height, width), 0)
    target = lax.broadcasted_iota(jnp.int32, (height, width), 1)
    token_ref[...] = jnp.zeros(token_ref.shape, F32)
    for batch in range(batches):
        table = jnp.zeros((height, width), F32)
        for t in range(TOGETHER):
            for l in range(SPREAD):
                first = (t * SPREAD + l) * 128
                lanes = jnp.logical_and(target >= first, target < first + 128)
                row = l * SIDE + batch * TOGETHER + t
                rows = jnp.logical_or(source == row, source == row + SPREAD * SIDE)
                table = jnp.where(jnp.logical_and(lanes, rows), 1.0, table)
        spread_ref[batch] = table.astype(BF16)


def turned(index, size, first):
    index = index - first
    return jnp.where(index < 0.0, index + size, index)


def parts_of(index, size):
    major = jnp.floor((index + 0.5) * (1.0 / size))
    return major, index - major * size


def row_lag_spot(index, n_row, n_lag):
    major, minor = parts_of(index, n_lag)
    return turned(major, n_row, ROW_FIRST) * n_lag + turned(minor, n_lag, LAG_FIRST)


def col_lag_spot(index, n_lag):
    major, minor = parts_of(index, n_lag)
    return major * n_lag + turned(minor, n_lag, LAG_FIRST)


def order_kernel(
    n_lag, copies, step_ref, hist_ref, rows_ref, cols_ref, mask_ref, token_ref, send_ref, picks_ref, hits_ref
):
    del token_ref
    lags = hist_ref.shape[0]
    lag_local = mask_ref.shape[0]
    lag = turned(iota((lags, lags), 0), lags, lags - LAG_FIRST * lag_local)
    slot = step_ref[...].astype(F32) - 1.0 - lag
    slot = jnp.where(slot < 0.0, slot + lags, slot)
    turn = jnp.where(slot == iota((lags, lags), 1), 1.0, 0.0).astype(BF16)
    high, mid, low = (jnp.dot(turn, part, preferred_element_type=F32) for part in split(hist_ref[...], 3))
    past = high + (mid + low)
    for k in range(copies):
        send_ref[pl.ds(k * lags, lags), :] = past

    cols = row_lag_spot(cols_ref[...].astype(F32), copies, n_lag) * lag_local
    spots = [jnp.where(mask_ref[pl.ds(l, 1), :] != 0, cols + l, -1.0) for l in range(lag_local)]
    picks_ref[...] = pick_rows(jnp.concatenate(spots, axis=1), picks_ref.shape[1])
    rows = as_column(col_lag_spot(rows_ref[...].astype(F32), n_lag), hits_ref.shape[1])
    hits_ref[...] = jnp.where(rows == iota(hits_ref.shape, 1), 1.0, 0.0)


def forward_kernel(
    n_row, n_col, n_lag, rows_ref, cols_ref, mask_ref, mats_ref, src_ref, picks_ref, hits_ref,
    out_ref, mirror_picks_ref, mirror_hits_ref, vecs,
):
    lag_local, pairs = mask_ref.shape
    block = src_ref.shape[1]
    own = n_lag * lag_local
    chunk = own + n_lag
    vecs[...] = select(picks_ref[...], src_ref[...])
    mine = lax.rem(lax.axis_index("row") + n_row - ROW_FIRST, n_row) * own
    group = src_ref[pl.ds(pl.multiple_of(mine, own), own), :]
    total = jnp.zeros((block, block), F32)
    for p in range(pairs):
        acc = mats_ref[p * lag_local] * vecs[pl.ds(p, 1), :]
        for l in range(1, lag_local):
            acc = acc + mats_ref[p * lag_local + l] * vecs[pl.ds(l * pairs + p, 1), :]
        total = total + jnp.sum(acc, axis=1, keepdims=True) * hits_ref[pl.ds(p, 1), :]
    fields = total.T
    for c in range(n_col):
        at = COL_ORDER.index(c) * chunk
        out_ref[pl.ds(at, own), :] = group
        out_ref[pl.ds(at + own, n_lag), :] = fields[c * n_lag : (c + 1) * n_lag]

    row_base = (lax.axis_index("row") * (n_col * n_lag)).astype(F32)
    col_base = (lax.axis_index("col") * n_lag).astype(F32)
    rows = rows_ref[...].astype(F32)
    cols = cols_ref[...].astype(F32)
    band, inner = parts_of(cols, n_lag)
    col_global = band * (n_col * n_lag) + col_base + inner
    off_diag = row_base + rows != col_global
    places = col_lag_spot(rows, n_lag) * lag_local
    spots = [
        jnp.where(jnp.logical_and(mask_ref[pl.ds(l, 1), :] != 0, off_diag), places + l, -1.0)
        for l in range(lag_local)
    ]
    ordered = [
        spots[l][:, g * SIDE : (g + 1) * SIDE] for g in range(pairs // SIDE) for l in range(lag_local)
    ]
    mirror_picks_ref[...] = pick_rows(jnp.concatenate(ordered, axis=1), mirror_picks_ref.shape[1])
    cols = jnp.concatenate([row_lag_spot(cols, n_row, n_lag)] * 8, axis=1)
    mirror_hits_ref[...] = jnp.where(cols == iota(mirror_hits_ref.shape, 0), 1.0, 0.0).astype(BF16)


def mirror_kernel(
    n_row, n_col, n_lag, lag_local, mats_ref, got_ref, picks_ref, hits_ref, spread_ref, out_ref, sides, whole, held
):
    pairs = hits_ref.shape[1] // 8
    block = got_ref.shape[1]
    terms = lag_local * pairs
    groups = pairs // SIDE
    per_group = SIDE * lag_local
    own = n_lag * lag_local
    chunk = own + n_lag
    group_past = jnp.concatenate([got_ref[pl.ds(COL_ORDER.index(c) * chunk, own), :] for c in range(n_col)], axis=0)
    columns = select(picks_ref[...], group_past).T
    whole[...] = columns
    high = columns.astype(BF16).astype(F32)
    low = columns - high
    for g in range(groups):
        keep = slice(g * per_group, g * per_group + SPREAD * SIDE)
        sides[g] = jnp.concatenate([high[:, keep], low[:, keep]], axis=1).astype(BF16)
    for g in range(groups):
        side = sides[g]
        for q in range(0, SIDE, TOGETHER):
            wide = jnp.dot(side, spread_ref[q // TOGETHER], preferred_element_type=F32)
            for t in range(TOGETHER):
                p = g * SIDE + q + t
                acc = jnp.zeros((8, block), F32)
                for l in range(lag_local):
                    if l < SPREAD:
                        first = (t * SPREAD + l) * block
                        factor = wide[:, first : first + block]
                    else:
                        lane = jnp.full((block, terms), g * per_group + l * SIDE + q + t, jnp.int32)
                        factor = jnp.take_along_axis(whole[...], lane, axis=1, mode="promise_in_bounds")
                    product = mats_ref[p * lag_local + l] * factor
                    acc = acc + jnp.sum(product.reshape(block // 8, 8, block), axis=0)
                held[pl.ds(p, 8, stride=pairs), :] = acc

    out_ref[...] = select(hits_ref[...], held[...])
    fields = got_ref[pl.ds(own, n_lag), :]
    for c in range(1, n_col):
        fields = fields + got_ref[pl.ds(c * chunk + own, n_lag), :]
    mine = lax.rem(lax.axis_index("row") + n_row - ROW_FIRST, n_row) * n_lag
    mine = pl.ds(pl.multiple_of(mine, n_lag), n_lag)
    out_ref[mine, :] = out_ref[mine, :] + fields


def final_kernel(got_ref, incident_ref, inverse_ref, out_ref):
    rhs = incident_ref[...] - jnp.sum(got_ref[...], axis=0, keepdims=True)
    sums = jnp.sum(inverse_ref[...] * rhs, axis=1, keepdims=True)
    shape = inverse_ref.shape
    out_ref[...] = jnp.sum(jnp.where(iota(shape, 0) == iota(shape, 1), sums, 0.0), axis=0, keepdims=True)


def call(kernel, name, outs, operands, limit, scratch=()):
    return pl.pallas_call(
        kernel,
        out_shape=tuple(jax.ShapeDtypeStruct(*out) for out in outs),
        in_specs=[VMEM] * len(operands),
        out_specs=tuple(VMEM for _ in outs),
        scratch_shapes=[pltpu.VMEM(*item) for item in scratch],
        name=name,
        compiler_params=pltpu.CompilerParams(vmem_limit_bytes=limit),
        cost_estimate=pl.CostEstimate(flops=20_000_000_000, bytes_accessed=64 * MIB, transcendentals=0),
    )(*operands)


def per_device(n_row, n_col, n_lag, history, step_index, pair_rows, pair_cols, lag_pattern, blocks, incident, self_inverse):
    lags = history.shape[0]
    block = history.shape[2]
    pairs = blocks.shape[2]
    lag_local = blocks.shape[3]
    terms = pairs * lag_local
    n_src = n_row * n_lag
    own = n_lag * lag_local
    chunk = own + n_lag
    rows = pair_rows.reshape(1, pairs)
    cols = pair_cols.reshape(1, pairs)
    mask = lag_pattern.reshape(pairs, lag_local).T
    mats = blocks.reshape(terms, block, block)

    spread, token = call(
        table_kernel,
        "table",
        [((SIDE // TOGETHER, 2 * SPREAD * SIDE, TOGETHER * SPREAD * block), BF16), ((8, block), F32)],
        [],
        MIB,
    )
    send, picks, hits = call(
        functools.partial(order_kernel, n_lag, n_row),
        "order",
        [((n_row * lags, block), F32), ((terms, n_row * lags), BF16), ((pairs, block), F32)],
        [step_index.reshape(1, 1), history.reshape(lags, block), rows, cols, mask, token],
        MIB,
    )
    row_lag_order = [
        (r + ROW_FIRST) % n_row * n_lag + (l + LAG_FIRST) % n_lag for r in range(n_row) for l in range(n_lag)
    ]
    source = lax.all_to_all(
        send.reshape(n_src, lag_local, block), ("row", "lag"), 0, 0, tiled=True, axis_index_groups=[row_lag_order]
    ).reshape(n_row * lags, block)
    sent, mirror_picks, mirror_hits = call(
        functools.partial(forward_kernel, n_row, n_col, n_lag),
        "forward",
        [((n_col * chunk, block), F32), ((terms, n_col * own), BF16), ((n_src, 8 * pairs), BF16)],
        [rows, cols, mask, mats, source, picks, hits],
        2 * MIB,
        [((terms, block), F32)],
    )
    got = lax.all_to_all(
        sent.reshape(n_col, chunk, block), "col", 0, 0, tiled=True, axis_index_groups=[list(COL_ORDER)]
    )
    (mirrored,) = call(
        functools.partial(mirror_kernel, n_row, n_col, n_lag, lag_local),
        "mirror",
        [((n_src, block), F32)],
        [mats, got.reshape(n_col * chunk, block), mirror_picks, mirror_hits, spread],
        3 * MIB,
        [
            ((pairs // SIDE, block, 2 * SPREAD * SIDE), BF16),
            ((block, terms), F32),
            ((8 * pairs, block), F32),
        ],
    )
    fields = lax.all_to_all(
        mirrored.reshape(n_src, 1, block), ("row", "lag"), 0, 0, tiled=True, axis_index_groups=[row_lag_order]
    )
    return call(
        final_kernel,
        "final",
        [((1, block), F32)],
        [fields.reshape(n_src, block), incident, self_inverse.reshape(block, block)],
        MIB,
    )[0]


def solution(mesh):
    in_specs = (
        P(None, ("row", "col", "lag"), None),
        P(),
        P("row", "col", None),
        P("row", "col", None),
        P("row", "col", None, "lag"),
        P("row", "col", None, "lag", None, None),
        P(("row", "col", "lag"), None),
        P(("row", "col", "lag"), None, None),
    )
    out_specs = P(("row", "col", "lag"), None)
    step = functools.partial(per_device, mesh.shape["row"], mesh.shape["col"], mesh.shape["lag"])
    return jax.shard_map(step, mesh=mesh, in_specs=in_specs, out_specs=out_specs, check_vma=False)
```

```python
import functools

import jax
import jax.numpy as jnp
from jax import lax
from jax.experimental import pallas as pl
from jax.experimental.pallas import tpu as pltpu
from jax.sharding import PartitionSpec as P

VMEM = pl.BlockSpec(memory_space=pltpu.VMEM)
F32 = jnp.float32
BF16 = jnp.bfloat16
MIB = 1024 * 1024
SIDE = 8
SPREAD = 3
TOGETHER = 2
COL_ORDER = (5, 4, 6, 3, 7, 2, 0, 1)
ROW_FIRST, LAG_FIRST = 2, 5


def iota(shape, dim):
    return lax.broadcasted_iota(jnp.int32, shape, dim).astype(F32)


def split(values, parts):
    pieces = []
    for _ in range(parts - 1):
        pieces.append(values.astype(BF16))
        values = values - pieces[-1].astype(F32)
    return pieces + [values.astype(BF16)]


def select(picks, values):
    return jnp.dot(
        jnp.concatenate([picks] * 2, axis=1), jnp.concatenate(split(values, 2), axis=0), preferred_element_type=F32
    )


def as_column(row, lanes):
    return jnp.broadcast_to(row, (lanes, row.shape[1])).T


def pick_rows(spots, width):
    at = as_column(spots, 128)
    at = jnp.concatenate([at] * (width // 128), axis=1)
    return jnp.where(at == iota(at.shape, 1), 1.0, 0.0).astype(BF16)


def table_kernel(spread_ref, token_ref):
    batches, height, width = spread_ref.shape
    source = lax.broadcasted_iota(jnp.int32, (height, width), 0)
    target = lax.broadcasted_iota(jnp.int32, (height, width), 1)
    token_ref[...] = jnp.zeros(token_ref.shape, F32)
    for batch in range(batches):
        table = jnp.zeros((height, width), F32)
        for t in range(TOGETHER):
            for l in range(SPREAD):
                first = (t * SPREAD + l) * 128
                lanes = jnp.logical_and(target >= first, target < first + 128)
                row = l * SIDE + batch * TOGETHER + t
                rows = jnp.logical_or(source == row, source == row + SPREAD * SIDE)
                table = jnp.where(jnp.logical_and(lanes, rows), 1.0, table)
        spread_ref[batch] = table.astype(BF16)


def turned(index, size, first):
    index = index - first
    return jnp.where(index < 0.0, index + size, index)


def parts_of(index, size):
    major = jnp.floor((index + 0.5) * (1.0 / size))
    return major, index - major * size


def row_lag_spot(index, n_row, n_lag):
    major, minor = parts_of(index, n_lag)
    return turned(major, n_row, ROW_FIRST) * n_lag + turned(minor, n_lag, LAG_FIRST)


def col_lag_spot(index, n_lag):
    major, minor = parts_of(index, n_lag)
    return major * n_lag + turned(minor, n_lag, LAG_FIRST)


def order_kernel(
    n_lag, copies, step_ref, hist_ref, rows_ref, cols_ref, mask_ref, token_ref, send_ref, picks_ref, hits_ref
):
    del token_ref
    lags = hist_ref.shape[0]
    lag_local = mask_ref.shape[0]
    lag = turned(iota((lags, lags), 0), lags, lags - LAG_FIRST * lag_local)
    slot = step_ref[...].astype(F32) - 1.0 - lag
    slot = jnp.where(slot < 0.0, slot + lags, slot)
    turn = jnp.where(slot == iota((lags, lags), 1), 1.0, 0.0).astype(BF16)
    high, mid, low = (jnp.dot(turn, part, preferred_element_type=F32) for part in split(hist_ref[...], 3))
    past = high + (mid + low)
    for k in range(copies):
        send_ref[pl.ds(k * lags, lags), :] = past

    cols = row_lag_spot(cols_ref[...].astype(F32), copies, n_lag) * lag_local
    spots = [jnp.where(mask_ref[pl.ds(l, 1), :] != 0, cols + l, -1.0) for l in range(lag_local)]
    picks_ref[...] = pick_rows(jnp.concatenate(spots, axis=1), picks_ref.shape[1])
    rows = as_column(col_lag_spot(rows_ref[...].astype(F32), n_lag), hits_ref.shape[1])
    hits_ref[...] = jnp.where(rows == iota(hits_ref.shape, 1), 1.0, 0.0)


def forward_kernel(
    n_row, n_col, n_lag, rows_ref, cols_ref, mask_ref, mats_ref, src_ref, picks_ref, hits_ref,
    out_ref, mirror_picks_ref, mirror_hits_ref, vecs,
):
    lag_local, pairs = mask_ref.shape
    block = src_ref.shape[1]
    own = n_lag * lag_local
    chunk = own + n_lag
    vecs[...] = select(picks_ref[...], src_ref[...])
    mine = lax.rem(lax.axis_index("row") + n_row - ROW_FIRST, n_row) * own
    group = src_ref[pl.ds(pl.multiple_of(mine, own), own), :]
    total = jnp.zeros((block, block), F32)
    for p in range(pairs):
        acc = mats_ref[p * lag_local] * vecs[pl.ds(p, 1), :]
        for l in range(1, lag_local):
            acc = acc + mats_ref[p * lag_local + l] * vecs[pl.ds(l * pairs + p, 1), :]
        total = total + jnp.sum(acc, axis=1, keepdims=True) * hits_ref[pl.ds(p, 1), :]
    fields = total.T
    for c in range(n_col):
        at = COL_ORDER.index(c) * chunk
        out_ref[pl.ds(at, own), :] = group
        out_ref[pl.ds(at + own, n_lag), :] = fields[c * n_lag : (c + 1) * n_lag]

    row_base = (lax.axis_index("row") * (n_col * n_lag)).astype(F32)
    col_base = (lax.axis_index("col") * n_lag).astype(F32)
    rows = rows_ref[...].astype(F32)
    cols = cols_ref[...].astype(F32)
    band, inner = parts_of(cols, n_lag)
    col_global = band * (n_col * n_lag) + col_base + inner
    off_diag = row_base + rows != col_global
    places = col_lag_spot(rows, n_lag) * lag_local
    spots = [
        jnp.where(jnp.logical_and(mask_ref[pl.ds(l, 1), :] != 0, off_diag), places + l, -1.0)
        for l in range(lag_local)
    ]
    ordered = [
        spots[l][:, g * SIDE : (g + 1) * SIDE] for g in range(pairs // SIDE) for l in range(lag_local)
    ]
    mirror_picks_ref[...] = pick_rows(jnp.concatenate(ordered, axis=1), mirror_picks_ref.shape[1])
    cols = jnp.concatenate([row_lag_spot(cols, n_row, n_lag)] * 8, axis=1)
    mirror_hits_ref[...] = jnp.where(cols == iota(mirror_hits_ref.shape, 0), 1.0, 0.0).astype(BF16)


def mirror_kernel(
    n_row, n_col, n_lag, lag_local, mats_ref, got_ref, picks_ref, hits_ref, spread_ref, out_ref, sides, held
):
    pairs = hits_ref.shape[1] // 8
    block = got_ref.shape[1]
    terms = lag_local * pairs
    groups = pairs // SIDE
    per_group = SIDE * lag_local
    own = n_lag * lag_local
    chunk = own + n_lag
    group_past = jnp.concatenate([got_ref[pl.ds(COL_ORDER.index(c) * chunk, own), :] for c in range(n_col)], axis=0)
    columns = select(picks_ref[...], group_past).T
    high = columns.astype(BF16).astype(F32)
    low = columns - high
    for g in range(groups):
        keep = slice(g * per_group, g * per_group + SPREAD * SIDE)
        sides[g] = jnp.concatenate([high[:, keep], low[:, keep]], axis=1).astype(BF16)
    for g in range(groups):
        side = sides[g]
        for q in range(0, SIDE, TOGETHER):
            wide = jnp.dot(side, spread_ref[q // TOGETHER], preferred_element_type=F32)
            for t in range(TOGETHER):
                p = g * SIDE + q + t
                acc = jnp.zeros((8, block), F32)
                for l in range(lag_local):
                    if l < SPREAD:
                        first = (t * SPREAD + l) * block
                        factor = wide[:, first : first + block]
                    else:
                        lane = jnp.full((block, terms), g * per_group + l * SIDE + q + t, jnp.int32)
                        factor = jnp.take_along_axis(columns, lane, axis=1, mode="promise_in_bounds")
                    product = mats_ref[p * lag_local + l] * factor
                    acc = acc + jnp.sum(product.reshape(block // 8, 8, block), axis=0)
                held[pl.ds(p, 8, stride=pairs), :] = acc

    out_ref[...] = select(hits_ref[...], held[...])
    fields = got_ref[pl.ds(own, n_lag), :]
    for c in range(1, n_col):
        fields = fields + got_ref[pl.ds(c * chunk + own, n_lag), :]
    mine = lax.rem(lax.axis_index("row") + n_row - ROW_FIRST, n_row) * n_lag
    mine = pl.ds(pl.multiple_of(mine, n_lag), n_lag)
    out_ref[mine, :] = out_ref[mine, :] + fields


def final_kernel(got_ref, incident_ref, inverse_ref, out_ref):
    rhs = incident_ref[...] - jnp.sum(got_ref[...], axis=0, keepdims=True)
    sums = jnp.sum(inverse_ref[...] * rhs, axis=1, keepdims=True)
    shape = inverse_ref.shape
    out_ref[...] = jnp.sum(jnp.where(iota(shape, 0) == iota(shape, 1), sums, 0.0), axis=0, keepdims=True)


def call(kernel, name, outs, operands, limit, scratch=(), flops=20 * 10**9):
    return pl.pallas_call(
        kernel,
        out_shape=tuple(jax.ShapeDtypeStruct(*out) for out in outs),
        in_specs=[VMEM] * len(operands),
        out_specs=tuple(VMEM for _ in outs),
        scratch_shapes=[pltpu.VMEM(*item) for item in scratch],
        name=name,
        compiler_params=pltpu.CompilerParams(vmem_limit_bytes=limit),
        cost_estimate=pl.CostEstimate(flops=flops, bytes_accessed=flops // 300, transcendentals=0),
    )(*operands)


def per_device(n_row, n_col, n_lag, history, step_index, pair_rows, pair_cols, lag_pattern, blocks, incident, self_inverse):
    lags = history.shape[0]
    block = history.shape[2]
    pairs = blocks.shape[2]
    lag_local = blocks.shape[3]
    terms = pairs * lag_local
    n_src = n_row * n_lag
    own = n_lag * lag_local
    chunk = own + n_lag
    rows = pair_rows.reshape(1, pairs)
    cols = pair_cols.reshape(1, pairs)
    mask = lag_pattern.reshape(pairs, lag_local).T
    mats = blocks.reshape(terms, block, block)

    spread, token = call(
        table_kernel,
        "table",
        [((SIDE // TOGETHER, 2 * SPREAD * SIDE, TOGETHER * SPREAD * block), BF16), ((8, block), F32)],
        [],
        MIB,
        flops=20000000000,
    )
    send, picks, hits = call(
        functools.partial(order_kernel, n_lag, n_row),
        "order",
        [((n_row * lags, block), F32), ((terms, n_row * lags), BF16), ((pairs, block), F32)],
        [step_index.reshape(1, 1), history.reshape(lags, block), rows, cols, mask, token],
        MIB,
        flops=200 * 10**9,
    )
    row_lag_order = [
        (r + ROW_FIRST) % n_row * n_lag + (l + LAG_FIRST) % n_lag for r in range(n_row) for l in range(n_lag)
    ]
    source = lax.all_to_all(
        send.reshape(n_src, lag_local, block), ("row", "lag"), 0, 0, tiled=True, axis_index_groups=[row_lag_order]
    ).reshape(n_row * lags, block)
    sent, mirror_picks, mirror_hits = call(
        functools.partial(forward_kernel, n_row, n_col, n_lag),
        "forward",
        [((n_col * chunk, block), F32), ((terms, n_col * own), BF16), ((n_src, 8 * pairs), BF16)],
        [rows, cols, mask, mats, source, picks, hits],
        2 * MIB,
        [((terms, block), F32)],
    )
    got = lax.all_to_all(
        sent.reshape(n_col, chunk, block), "col", 0, 0, tiled=True, axis_index_groups=[list(COL_ORDER)]
    )
    (mirrored,) = call(
        functools.partial(mirror_kernel, n_row, n_col, n_lag, lag_local),
        "mirror",
        [((n_src, block), F32)],
        [mats, got.reshape(n_col * chunk, block), mirror_picks, mirror_hits, spread],
        3 * MIB,
        [
            ((pairs // SIDE, block, 2 * SPREAD * SIDE), BF16),
            ((8 * pairs, block), F32),
        ],
    )
    fields = lax.all_to_all(
        mirrored.reshape(n_src, 1, block), ("row", "lag"), 0, 0, tiled=True, axis_index_groups=[row_lag_order]
    )
    return call(
        final_kernel,
        "final",
        [((1, block), F32)],
        [fields.reshape(n_src, block), incident, self_inverse.reshape(block, block)],
        MIB,
    )[0]


def solution(mesh):
    in_specs = (
        P(None, ("row", "col", "lag"), None),
        P(),
        P("row", "col", None),
        P("row", "col", None),
        P("row", "col", None, "lag"),
        P("row", "col", None, "lag", None, None),
        P(("row", "col", "lag"), None),
        P(("row", "col", "lag"), None, None),
    )
    out_specs = P(("row", "col", "lag"), None)
    step = functools.partial(per_device, mesh.shape["row"], mesh.shape["col"], mesh.shape["lag"])
    return jax.shard_map(step, mesh=mesh, in_specs=in_specs, out_specs=out_specs, check_vma=False)
```

```python
import functools

import jax
import jax.numpy as jnp
from jax import lax
from jax.experimental import pallas as pl
from jax.experimental.pallas import tpu as pltpu
from jax.sharding import PartitionSpec as P

VMEM = pl.BlockSpec(memory_space=pltpu.VMEM)
F32 = jnp.float32
BF16 = jnp.bfloat16
MIB = 1024 * 1024
PARTS = 3
SIDE = 8
SPREAD = 3
TOGETHER = 2
DEPTH = 80
COL_ORDER = (5, 4, 6, 3, 7, 2, 0, 1)
ROW_FIRST, LAG_FIRST = 2, 5


def iota(shape, dim):
    return lax.broadcasted_iota(jnp.int32, shape, dim).astype(F32)


def split(values):
    pieces = []
    for _ in range(PARTS - 1):
        pieces.append(values.astype(BF16))
        values = values - pieces[-1].astype(F32)
    return pieces + [values.astype(BF16)]


def select(picks, values):
    return jnp.dot(
        jnp.concatenate([picks] * PARTS, axis=1), jnp.concatenate(split(values), axis=0), preferred_element_type=F32
    )


def as_column(row, lanes):
    return jnp.broadcast_to(row, (lanes, row.shape[1])).T


def pick_rows(spots, width):
    at = as_column(spots, 128)
    at = jnp.concatenate([at] * (width // 128), axis=1)
    return jnp.where(at == iota(at.shape, 1), 1.0, 0.0).astype(BF16)


def table_kernel(spread_ref, token_ref):
    batches, height, width = spread_ref.shape
    source = lax.broadcasted_iota(jnp.int32, (height, width), 0)
    target = lax.broadcasted_iota(jnp.int32, (height, width), 1)
    token_ref[...] = jnp.zeros(token_ref.shape, F32)
    for batch in range(batches):
        table = jnp.zeros((height, width), F32)
        for t in range(TOGETHER):
            for l in range(SPREAD):
                first = (t * SPREAD + l) * 128
                lanes = jnp.logical_and(target >= first, target < first + 128)
                row = l * SIDE + batch * TOGETHER + t
                rows = source == row
                for part in range(1, PARTS):
                    rows = jnp.logical_or(rows, source == row + part * SPREAD * SIDE)
                table = jnp.where(jnp.logical_and(lanes, rows), 1.0, table)
        spread_ref[batch] = table.astype(BF16)


def turned(index, size, first):
    index = index - first
    return jnp.where(index < 0.0, index + size, index)


def parts_of(index, size):
    major = jnp.floor((index + 0.5) * (1.0 / size))
    return major, index - major * size


def row_lag_spot(index, n_row, n_lag):
    major, minor = parts_of(index, n_lag)
    return turned(major, n_row, ROW_FIRST) * n_lag + turned(minor, n_lag, LAG_FIRST)


def col_lag_spot(index, n_lag):
    major, minor = parts_of(index, n_lag)
    return major * n_lag + turned(minor, n_lag, LAG_FIRST)


def order_kernel(
    n_lag, copies, step_ref, hist_ref, rows_ref, cols_ref, mask_ref, token_ref, send_ref, picks_ref, hits_ref
):
    del token_ref
    lags = hist_ref.shape[0]
    lag_local = mask_ref.shape[0]
    lag = turned(iota((lags, lags), 0), lags, lags - LAG_FIRST * lag_local)
    slot = step_ref[...].astype(F32) - 1.0 - lag
    slot = jnp.where(slot < 0.0, slot + lags, slot)
    turn = jnp.where(slot == iota((lags, lags), 1), 1.0, 0.0).astype(BF16)
    high, mid, low = (jnp.dot(turn, part, preferred_element_type=F32) for part in split(hist_ref[...]))
    past = high + (mid + low)
    for k in range(copies):
        send_ref[pl.ds(k * lags, lags), :] = past

    cols = row_lag_spot(cols_ref[...].astype(F32), copies, n_lag) * lag_local
    spots = [jnp.where(mask_ref[pl.ds(l, 1), :] != 0, cols + l, -1.0) for l in range(lag_local)]
    picks_ref[...] = pick_rows(jnp.concatenate(spots, axis=1), picks_ref.shape[1])
    rows = as_column(col_lag_spot(rows_ref[...].astype(F32), n_lag), hits_ref.shape[1])
    hits_ref[...] = jnp.where(rows == iota(hits_ref.shape, 1), 1.0, 0.0)


def forward_kernel(
    n_row, n_col, n_lag, rows_ref, cols_ref, mask_ref, mats_ref, src_ref, picks_ref, hits_ref,
    out_ref, mirror_picks_ref, mirror_hits_ref, vecs,
):
    lag_local, pairs = mask_ref.shape
    block = src_ref.shape[1]
    own = n_lag * lag_local
    chunk = own + n_lag
    vecs[...] = select(picks_ref[...], src_ref[...])
    mine = lax.rem(lax.axis_index("row") + n_row - ROW_FIRST, n_row) * own
    group = src_ref[pl.ds(pl.multiple_of(mine, own), own), :]
    total = jnp.zeros((block, block), F32)
    for p in range(pairs):
        acc = mats_ref[p * lag_local] * vecs[pl.ds(p, 1), :]
        for l in range(1, lag_local):
            acc = acc + mats_ref[p * lag_local + l] * vecs[pl.ds(l * pairs + p, 1), :]
        total = total + jnp.sum(acc, axis=1, keepdims=True) * hits_ref[pl.ds(p, 1), :]
    fields = total.T
    for c in range(n_col):
        at = COL_ORDER.index(c) * chunk
        out_ref[pl.ds(at, own), :] = group
        out_ref[pl.ds(at + own, n_lag), :] = fields[c * n_lag : (c + 1) * n_lag]

    row_base = (lax.axis_index("row") * (n_col * n_lag)).astype(F32)
    col_base = (lax.axis_index("col") * n_lag).astype(F32)
    rows = rows_ref[...].astype(F32)
    cols = cols_ref[...].astype(F32)
    band, inner = parts_of(cols, n_lag)
    col_global = band * (n_col * n_lag) + col_base + inner
    off_diag = row_base + rows != col_global
    places = col_lag_spot(rows, n_lag) * lag_local
    spots = [
        jnp.where(jnp.logical_and(mask_ref[pl.ds(l, 1), :] != 0, off_diag), places + l, -1.0)
        for l in range(lag_local)
    ]
    ordered = [
        spots[l][:, g * SIDE : (g + 1) * SIDE] for g in range(pairs // SIDE) for l in range(lag_local)
    ]
    mirror_picks_ref[...] = pick_rows(jnp.concatenate(ordered, axis=1), mirror_picks_ref.shape[1])
    cols = jnp.concatenate([row_lag_spot(cols, n_row, n_lag)] * 8, axis=1)
    mirror_hits_ref[...] = jnp.where(cols == iota(mirror_hits_ref.shape, 0), 1.0, 0.0).astype(BF16)


def mirror_kernel(
    n_row, n_col, n_lag, lag_local, mats_ref, got_ref, picks_ref, hits_ref, spread_ref, out_ref, sides, held
):
    pairs = hits_ref.shape[1] // 8
    block = got_ref.shape[1]
    terms = lag_local * pairs
    groups = pairs // SIDE
    per_group = SIDE * lag_local
    own = n_lag * lag_local
    chunk = own + n_lag
    group_past = jnp.concatenate([got_ref[pl.ds(COL_ORDER.index(c) * chunk, own), :] for c in range(n_col)], axis=0)
    columns = select(picks_ref[...], group_past).T
    pieces = [piece.astype(F32) for piece in split(columns)]
    empty = jnp.zeros((block, DEPTH - PARTS * SPREAD * SIDE), F32)
    for g in range(groups):
        keep = slice(g * per_group, g * per_group + SPREAD * SIDE)
        sides[g] = jnp.concatenate([piece[:, keep] for piece in pieces] + [empty], axis=1).astype(BF16)
    for g in range(groups):
        side = sides[g]
        for q in range(0, SIDE, TOGETHER):
            wide = jnp.dot(side, spread_ref[q // TOGETHER], preferred_element_type=F32)
            for t in range(TOGETHER):
                p = g * SIDE + q + t
                acc = jnp.zeros((8, block), F32)
                for l in range(lag_local):
                    if l < SPREAD:
                        first = (t * SPREAD + l) * block
                        factor = wide[:, first : first + block]
                    else:
                        lane = jnp.full((block, terms), g * per_group + l * SIDE + q + t, jnp.int32)
                        factor = jnp.take_along_axis(columns, lane, axis=1, mode="promise_in_bounds")
                    product = mats_ref[p * lag_local + l] * factor
                    acc = acc + jnp.sum(product.reshape(block // 8, 8, block), axis=0)
                held[pl.ds(p, 8, stride=pairs), :] = acc

    out_ref[...] = select(hits_ref[...], held[...])
    fields = got_ref[pl.ds(own, n_lag), :]
    for c in range(1, n_col):
        fields = fields + got_ref[pl.ds(c * chunk + own, n_lag), :]
    mine = lax.rem(lax.axis_index("row") + n_row - ROW_FIRST, n_row) * n_lag
    mine = pl.ds(pl.multiple_of(mine, n_lag), n_lag)
    out_ref[mine, :] = out_ref[mine, :] + fields


def final_kernel(got_ref, incident_ref, inverse_ref, out_ref):
    rhs = incident_ref[...] - jnp.sum(got_ref[...], axis=0, keepdims=True)
    sums = jnp.sum(inverse_ref[...] * rhs, axis=1, keepdims=True)
    shape = inverse_ref.shape
    out_ref[...] = jnp.sum(jnp.where(iota(shape, 0) == iota(shape, 1), sums, 0.0), axis=0, keepdims=True)


def call(kernel, name, outs, operands, limit, scratch=(), flops=20 * 10**9):
    return pl.pallas_call(
        kernel,
        out_shape=tuple(jax.ShapeDtypeStruct(*out) for out in outs),
        in_specs=[VMEM] * len(operands),
        out_specs=tuple(VMEM for _ in outs),
        scratch_shapes=[pltpu.VMEM(*item) for item in scratch],
        name=name,
        compiler_params=pltpu.CompilerParams(vmem_limit_bytes=limit),
        cost_estimate=pl.CostEstimate(flops=flops, bytes_accessed=flops // 300, transcendentals=0),
    )(*operands)


def per_device(n_row, n_col, n_lag, history, step_index, pair_rows, pair_cols, lag_pattern, blocks, incident, self_inverse):
    lags = history.shape[0]
    block = history.shape[2]
    pairs = blocks.shape[2]
    lag_local = blocks.shape[3]
    terms = pairs * lag_local
    n_src = n_row * n_lag
    own = n_lag * lag_local
    chunk = own + n_lag
    rows = pair_rows.reshape(1, pairs)
    cols = pair_cols.reshape(1, pairs)
    mask = lag_pattern.reshape(pairs, lag_local).T
    mats = blocks.reshape(terms, block, block)

    spread, token = call(
        table_kernel,
        "table",
        [((SIDE // TOGETHER, DEPTH, TOGETHER * SPREAD * block), BF16), ((8, block), F32)],
        [],
        MIB,
        flops=20000000000,
    )
    send, picks, hits = call(
        functools.partial(order_kernel, n_lag, n_row),
        "order",
        [((n_row * lags, block), F32), ((terms, n_row * lags), BF16), ((pairs, block), F32)],
        [step_index.reshape(1, 1), history.reshape(lags, block), rows, cols, mask, token],
        MIB,
        flops=200 * 10**9,
    )
    row_lag_order = [
        (r + ROW_FIRST) % n_row * n_lag + (l + LAG_FIRST) % n_lag for r in range(n_row) for l in range(n_lag)
    ]
    source = lax.all_to_all(
        send.reshape(n_src, lag_local, block), ("row", "lag"), 0, 0, tiled=True, axis_index_groups=[row_lag_order]
    ).reshape(n_row * lags, block)
    sent, mirror_picks, mirror_hits = call(
        functools.partial(forward_kernel, n_row, n_col, n_lag),
        "forward",
        [((n_col * chunk, block), F32), ((terms, n_col * own), BF16), ((n_src, 8 * pairs), BF16)],
        [rows, cols, mask, mats, source, picks, hits],
        2 * MIB,
        [((terms, block), F32)],
    )
    got = lax.all_to_all(
        sent.reshape(n_col, chunk, block), "col", 0, 0, tiled=True, axis_index_groups=[list(COL_ORDER)]
    )
    (mirrored,) = call(
        functools.partial(mirror_kernel, n_row, n_col, n_lag, lag_local),
        "mirror",
        [((n_src, block), F32)],
        [mats, got.reshape(n_col * chunk, block), mirror_picks, mirror_hits, spread],
        3 * MIB,
        [
            ((pairs // SIDE, block, DEPTH), BF16),
            ((8 * pairs, block), F32),
        ],
    )
    fields = lax.all_to_all(
        mirrored.reshape(n_src, 1, block), ("row", "lag"), 0, 0, tiled=True, axis_index_groups=[row_lag_order]
    )
    return call(
        final_kernel,
        "final",
        [((1, block), F32)],
        [fields.reshape(n_src, block), incident, self_inverse.reshape(block, block)],
        MIB,
    )[0]


def solution(mesh):
    in_specs = (
        P(None, ("row", "col", "lag"), None),
        P(),
        P("row", "col", None),
        P("row", "col", None),
        P("row", "col", None, "lag"),
        P("row", "col", None, "lag", None, None),
        P(("row", "col", "lag"), None),
        P(("row", "col", "lag"), None, None),
    )
    out_specs = P(("row", "col", "lag"), None)
    step = functools.partial(per_device, mesh.shape["row"], mesh.shape["col"], mesh.shape["lag"])
    return jax.shard_map(step, mesh=mesh, in_specs=in_specs, out_specs=out_specs, check_vma=False)
```

```python
import functools

import jax
import jax.numpy as jnp
from jax import lax
from jax.experimental import pallas as pl
from jax.experimental.pallas import tpu as pltpu
from jax.sharding import PartitionSpec as P

VMEM = pl.BlockSpec(memory_space=pltpu.VMEM)
F32 = jnp.float32
BF16 = jnp.bfloat16
MIB = 1024 * 1024
PARTS = 3
SIDE = 8
SPREAD = 3
TOGETHER = 2
DEPTH = 80
COL_ORDER = (5, 4, 6, 3, 7, 2, 0, 1)
ROW_FIRST, LAG_FIRST = 2, 5


def iota(shape, dim):
    return lax.broadcasted_iota(jnp.int32, shape, dim).astype(F32)


def split(values):
    pieces = []
    for _ in range(PARTS - 1):
        pieces.append(values.astype(BF16))
        values = values - pieces[-1].astype(F32)
    return pieces + [values.astype(BF16)]


def select(picks, values):
    return jnp.dot(
        jnp.concatenate([picks] * PARTS, axis=1), jnp.concatenate(split(values), axis=0), preferred_element_type=F32
    )


def as_column(row, lanes):
    return jnp.broadcast_to(row, (lanes, row.shape[1])).T


def pick_rows(spots, width):
    at = as_column(spots, 128)
    at = jnp.concatenate([at] * (width // 128), axis=1)
    return jnp.where(at == iota(at.shape, 1), 1.0, 0.0).astype(BF16)


def table_kernel(spread_ref, token_ref):
    batches, height, width = spread_ref.shape
    source = lax.broadcasted_iota(jnp.int32, (height, width), 0)
    target = lax.broadcasted_iota(jnp.int32, (height, width), 1)
    token_ref[...] = jnp.zeros(token_ref.shape, F32)
    for batch in range(batches):
        table = jnp.zeros((height, width), F32)
        for t in range(TOGETHER):
            for l in range(SPREAD):
                first = (t * SPREAD + l) * 128
                lanes = jnp.logical_and(target >= first, target < first + 128)
                row = l * SIDE + batch * TOGETHER + t
                rows = source == row
                for part in range(1, PARTS):
                    rows = jnp.logical_or(rows, source == row + part * SPREAD * SIDE)
                table = jnp.where(jnp.logical_and(lanes, rows), 1.0, table)
        spread_ref[batch] = table.astype(BF16)


def turned(index, size, first):
    index = index - first
    return jnp.where(index < 0.0, index + size, index)


def parts_of(index, size):
    major = jnp.floor((index + 0.5) * (1.0 / size))
    return major, index - major * size


def row_lag_spot(index, n_row, n_lag):
    major, minor = parts_of(index, n_lag)
    return turned(major, n_row, ROW_FIRST) * n_lag + turned(minor, n_lag, LAG_FIRST)


def col_lag_spot(index, n_lag):
    major, minor = parts_of(index, n_lag)
    return major * n_lag + turned(minor, n_lag, LAG_FIRST)


def order_kernel(
    n_lag, copies, step_ref, hist_ref, rows_ref, cols_ref, mask_ref, token_ref, send_ref, picks_ref, hits_ref
):
    del token_ref
    lags = hist_ref.shape[0]
    lag_local = mask_ref.shape[0]
    lag = turned(iota((lags, lags), 0), lags, lags - LAG_FIRST * lag_local)
    slot = step_ref[...].astype(F32) - 1.0 - lag
    slot = jnp.where(slot < 0.0, slot + lags, slot)
    turn = jnp.where(slot == iota((lags, lags), 1), 1.0, 0.0).astype(BF16)
    high, mid, low = (jnp.dot(turn, part, preferred_element_type=F32) for part in split(hist_ref[...]))
    past = high + (mid + low)
    for k in range(copies):
        send_ref[pl.ds(k * lags, lags), :] = past

    cols = row_lag_spot(cols_ref[...].astype(F32), copies, n_lag) * lag_local
    spots = [jnp.where(mask_ref[pl.ds(l, 1), :] != 0, cols + l, -1.0) for l in range(lag_local)]
    picks_ref[...] = pick_rows(jnp.concatenate(spots, axis=1), picks_ref.shape[1])
    rows = as_column(col_lag_spot(rows_ref[...].astype(F32), n_lag), hits_ref.shape[1])
    hits_ref[...] = jnp.where(rows == iota(hits_ref.shape, 1), 1.0, 0.0)


def forward_kernel(
    n_row, n_col, n_lag, rows_ref, cols_ref, mask_ref, mats_ref, src_ref, picks_ref, hits_ref,
    out_ref, mirror_picks_ref, mirror_hits_ref, vecs,
):
    lag_local, pairs = mask_ref.shape
    block = src_ref.shape[1]
    own = n_lag * lag_local
    chunk = own + n_lag
    vecs[...] = select(picks_ref[...], src_ref[...])
    mine = lax.rem(lax.axis_index("row") + n_row - ROW_FIRST, n_row) * own
    group = src_ref[pl.ds(pl.multiple_of(mine, own), own), :]
    total = jnp.zeros((block, block), F32)
    for p in range(pairs):
        acc = mats_ref[p * lag_local] * vecs[pl.ds(p, 1), :]
        for l in range(1, lag_local):
            acc = acc + mats_ref[p * lag_local + l] * vecs[pl.ds(l * pairs + p, 1), :]
        total = total + jnp.sum(acc, axis=1, keepdims=True) * hits_ref[pl.ds(p, 1), :]
    fields = total.T
    for c in range(n_col):
        at = COL_ORDER.index(c) * chunk
        out_ref[pl.ds(at, own), :] = group
        out_ref[pl.ds(at + own, n_lag), :] = fields[c * n_lag : (c + 1) * n_lag]

    row_base = (lax.axis_index("row") * (n_col * n_lag)).astype(F32)
    col_base = (lax.axis_index("col") * n_lag).astype(F32)
    rows = rows_ref[...].astype(F32)
    cols = cols_ref[...].astype(F32)
    band, inner = parts_of(cols, n_lag)
    col_global = band * (n_col * n_lag) + col_base + inner
    off_diag = row_base + rows != col_global
    places = col_lag_spot(rows, n_lag) * lag_local
    spots = [
        jnp.where(jnp.logical_and(mask_ref[pl.ds(l, 1), :] != 0, off_diag), places + l, -1.0)
        for l in range(lag_local)
    ]
    ordered = [
        spots[l][:, g * SIDE : (g + 1) * SIDE] for g in range(pairs // SIDE) for l in range(lag_local)
    ]
    mirror_picks_ref[...] = pick_rows(jnp.concatenate(ordered, axis=1), mirror_picks_ref.shape[1])
    cols = row_lag_spot(cols, n_row, n_lag)
    mirror_hits_ref[...] = jnp.where(cols == iota(mirror_hits_ref.shape, 0), 1.0, 0.0).astype(BF16)


def mirror_kernel(
    n_row, n_col, n_lag, lag_local, mats_ref, got_ref, picks_ref, hits_ref, spread_ref, out_ref, sides, held
):
    pairs = hits_ref.shape[1]
    block = got_ref.shape[1]
    terms = lag_local * pairs
    groups = pairs // SIDE
    per_group = SIDE * lag_local
    own = n_lag * lag_local
    chunk = own + n_lag
    group_past = jnp.concatenate([got_ref[pl.ds(COL_ORDER.index(c) * chunk, own), :] for c in range(n_col)], axis=0)
    columns = select(picks_ref[...], group_past).T
    pieces = [piece.astype(F32) for piece in split(columns)]
    empty = jnp.zeros((block, DEPTH - PARTS * SPREAD * SIDE), F32)
    for g in range(groups):
        keep = slice(g * per_group, g * per_group + SPREAD * SIDE)
        sides[g] = jnp.concatenate([piece[:, keep] for piece in pieces] + [empty], axis=1).astype(BF16)
    for g in range(groups):
        side = sides[g]
        for q in range(0, SIDE, TOGETHER):
            wide = jnp.dot(side, spread_ref[q // TOGETHER], preferred_element_type=F32)
            for t in range(TOGETHER):
                p = g * SIDE + q + t
                acc = jnp.zeros((8, block), F32)
                for l in range(lag_local):
                    if l < SPREAD:
                        first = (t * SPREAD + l) * block
                        factor = wide[:, first : first + block]
                    else:
                        lane = jnp.full((block, terms), g * per_group + l * SIDE + q + t, jnp.int32)
                        factor = jnp.take_along_axis(columns, lane, axis=1, mode="promise_in_bounds")
                    product = mats_ref[p * lag_local + l] * factor
                    acc = acc + jnp.sum(product.reshape(block // 8, 8, block), axis=0)
                held[pl.ds(p, 8, stride=pairs), :] = acc

    out_ref[...] = select(hits_ref[...], jnp.sum(held[...].reshape(8, pairs, block), axis=0))
    fields = got_ref[pl.ds(own, n_lag), :]
    for c in range(1, n_col):
        fields = fields + got_ref[pl.ds(c * chunk + own, n_lag), :]
    mine = lax.rem(lax.axis_index("row") + n_row - ROW_FIRST, n_row) * n_lag
    mine = pl.ds(pl.multiple_of(mine, n_lag), n_lag)
    out_ref[mine, :] = out_ref[mine, :] + fields


def final_kernel(got_ref, incident_ref, inverse_ref, out_ref):
    rhs = incident_ref[...] - jnp.sum(got_ref[...], axis=0, keepdims=True)
    sums = jnp.sum(inverse_ref[...] * rhs, axis=1, keepdims=True)
    shape = inverse_ref.shape
    out_ref[...] = jnp.sum(jnp.where(iota(shape, 0) == iota(shape, 1), sums, 0.0), axis=0, keepdims=True)


def call(kernel, name, outs, operands, limit, scratch=(), flops=20 * 10**9):
    return pl.pallas_call(
        kernel,
        out_shape=tuple(jax.ShapeDtypeStruct(*out) for out in outs),
        in_specs=[VMEM] * len(operands),
        out_specs=tuple(VMEM for _ in outs),
        scratch_shapes=[pltpu.VMEM(*item) for item in scratch],
        name=name,
        compiler_params=pltpu.CompilerParams(vmem_limit_bytes=limit),
        cost_estimate=pl.CostEstimate(flops=flops, bytes_accessed=flops // 300, transcendentals=0),
    )(*operands)


def per_device(n_row, n_col, n_lag, history, step_index, pair_rows, pair_cols, lag_pattern, blocks, incident, self_inverse):
    lags = history.shape[0]
    block = history.shape[2]
    pairs = blocks.shape[2]
    lag_local = blocks.shape[3]
    terms = pairs * lag_local
    n_src = n_row * n_lag
    own = n_lag * lag_local
    chunk = own + n_lag
    rows = pair_rows.reshape(1, pairs)
    cols = pair_cols.reshape(1, pairs)
    mask = lag_pattern.reshape(pairs, lag_local).T
    mats = blocks.reshape(terms, block, block)

    spread, token = call(
        table_kernel,
        "table",
        [((SIDE // TOGETHER, DEPTH, TOGETHER * SPREAD * block), BF16), ((8, block), F32)],
        [],
        MIB,
        flops=20000000000,
    )
    send, picks, hits = call(
        functools.partial(order_kernel, n_lag, n_row),
        "order",
        [((n_row * lags, block), F32), ((terms, n_row * lags), BF16), ((pairs, block), F32)],
        [step_index.reshape(1, 1), history.reshape(lags, block), rows, cols, mask, token],
        MIB,
        flops=200 * 10**9,
    )
    row_lag_order = [
        (r + ROW_FIRST) % n_row * n_lag + (l + LAG_FIRST) % n_lag for r in range(n_row) for l in range(n_lag)
    ]
    source = lax.all_to_all(
        send.reshape(n_src, lag_local, block), ("row", "lag"), 0, 0, tiled=True, axis_index_groups=[row_lag_order]
    ).reshape(n_row * lags, block)
    sent, mirror_picks, mirror_hits = call(
        functools.partial(forward_kernel, n_row, n_col, n_lag),
        "forward",
        [((n_col * chunk, block), F32), ((terms, n_col * own), BF16), ((n_src, pairs), BF16)],
        [rows, cols, mask, mats, source, picks, hits],
        2 * MIB,
        [((terms, block), F32)],
    )
    got = lax.all_to_all(
        sent.reshape(n_col, chunk, block), "col", 0, 0, tiled=True, axis_index_groups=[list(COL_ORDER)]
    )
    (mirrored,) = call(
        functools.partial(mirror_kernel, n_row, n_col, n_lag, lag_local),
        "mirror",
        [((n_src, block), F32)],
        [mats, got.reshape(n_col * chunk, block), mirror_picks, mirror_hits, spread],
        3 * MIB,
        [
            ((pairs // SIDE, block, DEPTH), BF16),
            ((8 * pairs, block), F32),
        ],
    )
    fields = lax.all_to_all(
        mirrored.reshape(n_src, 1, block), ("row", "lag"), 0, 0, tiled=True, axis_index_groups=[row_lag_order]
    )
    return call(
        final_kernel,
        "final",
        [((1, block), F32)],
        [fields.reshape(n_src, block), incident, self_inverse.reshape(block, block)],
        MIB,
    )[0]


def solution(mesh):
    in_specs = (
        P(None, ("row", "col", "lag"), None),
        P(),
        P("row", "col", None),
        P("row", "col", None),
        P("row", "col", None, "lag"),
        P("row", "col", None, "lag", None, None),
        P(("row", "col", "lag"), None),
        P(("row", "col", "lag"), None, None),
    )
    out_specs = P(("row", "col", "lag"), None)
    step = functools.partial(per_device, mesh.shape["row"], mesh.shape["col"], mesh.shape["lag"])
    return jax.shard_map(step, mesh=mesh, in_specs=in_specs, out_specs=out_specs, check_vma=False)
```

```python
import functools

import jax
import jax.numpy as jnp
from jax import lax
from jax.experimental import pallas as pl
from jax.experimental.pallas import tpu as pltpu
from jax.sharding import PartitionSpec as P

VMEM = pl.BlockSpec(memory_space=pltpu.VMEM)
F32 = jnp.float32
BF16 = jnp.bfloat16
MIB = 1024 * 1024
PARTS = 3
SIDE = 8
SPREAD = 3
TOGETHER = 4
DEPTH = 80
COL_ORDER = (5, 4, 6, 3, 7, 2, 0, 1)
ROW_FIRST, LAG_FIRST = 2, 5


def iota(shape, dim):
    return lax.broadcasted_iota(jnp.int32, shape, dim).astype(F32)


def split(values):
    pieces = []
    for _ in range(PARTS - 1):
        pieces.append(values.astype(BF16))
        values = values - pieces[-1].astype(F32)
    return pieces + [values.astype(BF16)]


def select(picks, values):
    return jnp.dot(
        jnp.concatenate([picks] * PARTS, axis=1), jnp.concatenate(split(values), axis=0), preferred_element_type=F32
    )


def as_column(row, lanes):
    return jnp.broadcast_to(row, (lanes, row.shape[1])).T


def pick_rows(spots, width):
    at = as_column(spots, 128)
    at = jnp.concatenate([at] * (width // 128), axis=1)
    return jnp.where(at == iota(at.shape, 1), 1.0, 0.0).astype(BF16)


def table_kernel(spread_ref, token_ref):
    batches, height, width = spread_ref.shape
    source = lax.broadcasted_iota(jnp.int32, (height, width), 0)
    target = lax.broadcasted_iota(jnp.int32, (height, width), 1)
    token_ref[...] = jnp.zeros(token_ref.shape, F32)
    for batch in range(batches):
        table = jnp.zeros((height, width), F32)
        for t in range(TOGETHER):
            for l in range(SPREAD):
                first = (t * SPREAD + l) * 128
                lanes = jnp.logical_and(target >= first, target < first + 128)
                row = l * SIDE + batch * TOGETHER + t
                rows = source == row
                for part in range(1, PARTS):
                    rows = jnp.logical_or(rows, source == row + part * SPREAD * SIDE)
                table = jnp.where(jnp.logical_and(lanes, rows), 1.0, table)
        spread_ref[batch] = table.astype(BF16)


def turned(index, size, first):
    index = index - first
    return jnp.where(index < 0.0, index + size, index)


def parts_of(index, size):
    major = jnp.floor((index + 0.5) * (1.0 / size))
    return major, index - major * size


def row_lag_spot(index, n_row, n_lag):
    major, minor = parts_of(index, n_lag)
    return turned(major, n_row, ROW_FIRST) * n_lag + turned(minor, n_lag, LAG_FIRST)


def col_lag_spot(index, n_lag):
    major, minor = parts_of(index, n_lag)
    return major * n_lag + turned(minor, n_lag, LAG_FIRST)


def order_kernel(
    n_lag, copies, step_ref, hist_ref, rows_ref, cols_ref, mask_ref, token_ref, send_ref, picks_ref, hits_ref
):
    del token_ref
    lags = hist_ref.shape[0]
    lag_local = mask_ref.shape[0]
    lag = turned(iota((lags, lags), 0), lags, lags - LAG_FIRST * lag_local)
    slot = step_ref[...].astype(F32) - 1.0 - lag
    slot = jnp.where(slot < 0.0, slot + lags, slot)
    turn = jnp.where(slot == iota((lags, lags), 1), 1.0, 0.0).astype(BF16)
    high, mid, low = (jnp.dot(turn, part, preferred_element_type=F32) for part in split(hist_ref[...]))
    past = high + (mid + low)
    for k in range(copies):
        send_ref[pl.ds(k * lags, lags), :] = past

    cols = row_lag_spot(cols_ref[...].astype(F32), copies, n_lag) * lag_local
    spots = [jnp.where(mask_ref[pl.ds(l, 1), :] != 0, cols + l, -1.0) for l in range(lag_local)]
    picks_ref[...] = pick_rows(jnp.concatenate(spots, axis=1), picks_ref.shape[1])
    rows = as_column(col_lag_spot(rows_ref[...].astype(F32), n_lag), hits_ref.shape[1])
    hits_ref[...] = jnp.where(rows == iota(hits_ref.shape, 1), 1.0, 0.0)


def forward_kernel(
    n_row, n_col, n_lag, rows_ref, cols_ref, mask_ref, mats_ref, src_ref, picks_ref, hits_ref,
    out_ref, mirror_picks_ref, mirror_hits_ref, vecs,
):
    lag_local, pairs = mask_ref.shape
    block = src_ref.shape[1]
    own = n_lag * lag_local
    chunk = own + n_lag
    vecs[...] = select(picks_ref[...], src_ref[...])
    mine = lax.rem(lax.axis_index("row") + n_row - ROW_FIRST, n_row) * own
    group = src_ref[pl.ds(pl.multiple_of(mine, own), own), :]
    total = jnp.zeros((block, block), F32)
    for p in range(pairs):
        acc = mats_ref[p * lag_local] * vecs[pl.ds(p, 1), :]
        for l in range(1, lag_local):
            acc = acc + mats_ref[p * lag_local + l] * vecs[pl.ds(l * pairs + p, 1), :]
        total = total + jnp.sum(acc, axis=1, keepdims=True) * hits_ref[pl.ds(p, 1), :]
    fields = total.T
    for c in range(n_col):
        at = COL_ORDER.index(c) * chunk
        out_ref[pl.ds(at, own), :] = group
        out_ref[pl.ds(at + own, n_lag), :] = fields[c * n_lag : (c + 1) * n_lag]

    row_base = (lax.axis_index("row") * (n_col * n_lag)).astype(F32)
    col_base = (lax.axis_index("col") * n_lag).astype(F32)
    rows = rows_ref[...].astype(F32)
    cols = cols_ref[...].astype(F32)
    band, inner = parts_of(cols, n_lag)
    col_global = band * (n_col * n_lag) + col_base + inner
    off_diag = row_base + rows != col_global
    places = col_lag_spot(rows, n_lag) * lag_local
    spots = [
        jnp.where(jnp.logical_and(mask_ref[pl.ds(l, 1), :] != 0, off_diag), places + l, -1.0)
        for l in range(lag_local)
    ]
    ordered = [
        spots[l][:, g * SIDE : (g + 1) * SIDE] for g in range(pairs // SIDE) for l in range(lag_local)
    ]
    mirror_picks_ref[...] = pick_rows(jnp.concatenate(ordered, axis=1), mirror_picks_ref.shape[1])
    cols = jnp.concatenate([row_lag_spot(cols, n_row, n_lag)] * 8, axis=1)
    mirror_hits_ref[...] = jnp.where(cols == iota(mirror_hits_ref.shape, 0), 1.0, 0.0).astype(BF16)


def mirror_kernel(
    n_row, n_col, n_lag, lag_local, mats_ref, got_ref, picks_ref, hits_ref, spread_ref, out_ref, sides, held
):
    pairs = hits_ref.shape[1] // 8
    block = got_ref.shape[1]
    terms = lag_local * pairs
    groups = pairs // SIDE
    per_group = SIDE * lag_local
    own = n_lag * lag_local
    chunk = own + n_lag
    group_past = jnp.concatenate([got_ref[pl.ds(COL_ORDER.index(c) * chunk, own), :] for c in range(n_col)], axis=0)
    columns = select(picks_ref[...], group_past).T
    pieces = [piece.astype(F32) for piece in split(columns)]
    empty = jnp.zeros((block, DEPTH - PARTS * SPREAD * SIDE), F32)
    for g in range(groups):
        keep = slice(g * per_group, g * per_group + SPREAD * SIDE)
        sides[g] = jnp.concatenate([piece[:, keep] for piece in pieces] + [empty], axis=1).astype(BF16)
    for g in range(groups):
        side = sides[g]
        for q in range(0, SIDE, TOGETHER):
            wide = jnp.dot(side, spread_ref[q // TOGETHER], preferred_element_type=F32)
            for t in range(TOGETHER):
                p = g * SIDE + q + t
                acc = jnp.zeros((8, block), F32)
                for l in range(lag_local):
                    if l < SPREAD:
                        first = (t * SPREAD + l) * block
                        factor = wide[:, first : first + block]
                    else:
                        lane = jnp.full((block, terms), g * per_group + l * SIDE + q + t, jnp.int32)
                        factor = jnp.take_along_axis(columns, lane, axis=1, mode="promise_in_bounds")
                    product = mats_ref[p * lag_local + l] * factor
                    acc = acc + jnp.sum(product.reshape(block // 8, 8, block), axis=0)
                held[pl.ds(p, 8, stride=pairs), :] = acc

    out_ref[...] = select(hits_ref[...], held[...])
    fields = got_ref[pl.ds(own, n_lag), :]
    for c in range(1, n_col):
        fields = fields + got_ref[pl.ds(c * chunk + own, n_lag), :]
    mine = lax.rem(lax.axis_index("row") + n_row - ROW_FIRST, n_row) * n_lag
    mine = pl.ds(pl.multiple_of(mine, n_lag), n_lag)
    out_ref[mine, :] = out_ref[mine, :] + fields


def final_kernel(got_ref, incident_ref, inverse_ref, out_ref):
    rhs = incident_ref[...] - jnp.sum(got_ref[...], axis=0, keepdims=True)
    sums = jnp.sum(inverse_ref[...] * rhs, axis=1, keepdims=True)
    shape = inverse_ref.shape
    out_ref[...] = jnp.sum(jnp.where(iota(shape, 0) == iota(shape, 1), sums, 0.0), axis=0, keepdims=True)


def call(kernel, name, outs, operands, limit, scratch=(), flops=20 * 10**9):
    return pl.pallas_call(
        kernel,
        out_shape=tuple(jax.ShapeDtypeStruct(*out) for out in outs),
        in_specs=[VMEM] * len(operands),
        out_specs=tuple(VMEM for _ in outs),
        scratch_shapes=[pltpu.VMEM(*item) for item in scratch],
        name=name,
        compiler_params=pltpu.CompilerParams(vmem_limit_bytes=limit),
        cost_estimate=pl.CostEstimate(flops=flops, bytes_accessed=flops // 300, transcendentals=0),
    )(*operands)


def per_device(n_row, n_col, n_lag, history, step_index, pair_rows, pair_cols, lag_pattern, blocks, incident, self_inverse):
    lags = history.shape[0]
    block = history.shape[2]
    pairs = blocks.shape[2]
    lag_local = blocks.shape[3]
    terms = pairs * lag_local
    n_src = n_row * n_lag
    own = n_lag * lag_local
    chunk = own + n_lag
    rows = pair_rows.reshape(1, pairs)
    cols = pair_cols.reshape(1, pairs)
    mask = lag_pattern.reshape(pairs, lag_local).T
    mats = blocks.reshape(terms, block, block)

    spread, token = call(
        table_kernel,
        "table",
        [((SIDE // TOGETHER, DEPTH, TOGETHER * SPREAD * block), BF16), ((8, block), F32)],
        [],
        MIB,
        flops=20000000000,
    )
    send, picks, hits = call(
        functools.partial(order_kernel, n_lag, n_row),
        "order",
        [((n_row * lags, block), F32), ((terms, n_row * lags), BF16), ((pairs, block), F32)],
        [step_index.reshape(1, 1), history.reshape(lags, block), rows, cols, mask, token],
        MIB,
        flops=200 * 10**9,
    )
    row_lag_order = [
        (r + ROW_FIRST) % n_row * n_lag + (l + LAG_FIRST) % n_lag for r in range(n_row) for l in range(n_lag)
    ]
    source = lax.all_to_all(
        send.reshape(n_src, lag_local, block), ("row", "lag"), 0, 0, tiled=True, axis_index_groups=[row_lag_order]
    ).reshape(n_row * lags, block)
    sent, mirror_picks, mirror_hits = call(
        functools.partial(forward_kernel, n_row, n_col, n_lag),
        "forward",
        [((n_col * chunk, block), F32), ((terms, n_col * own), BF16), ((n_src, 8 * pairs), BF16)],
        [rows, cols, mask, mats, source, picks, hits],
        2 * MIB,
        [((terms, block), F32)],
    )
    got = lax.all_to_all(
        sent.reshape(n_col, chunk, block), "col", 0, 0, tiled=True, axis_index_groups=[list(COL_ORDER)]
    )
    (mirrored,) = call(
        functools.partial(mirror_kernel, n_row, n_col, n_lag, lag_local),
        "mirror",
        [((n_src, block), F32)],
        [mats, got.reshape(n_col * chunk, block), mirror_picks, mirror_hits, spread],
        3 * MIB,
        [
            ((pairs // SIDE, block, DEPTH), BF16),
            ((8 * pairs, block), F32),
        ],
    )
    fields = lax.all_to_all(
        mirrored.reshape(n_src, 1, block), ("row", "lag"), 0, 0, tiled=True, axis_index_groups=[row_lag_order]
    )
    return call(
        final_kernel,
        "final",
        [((1, block), F32)],
        [fields.reshape(n_src, block), incident, self_inverse.reshape(block, block)],
        MIB,
    )[0]


def solution(mesh):
    in_specs = (
        P(None, ("row", "col", "lag"), None),
        P(),
        P("row", "col", None),
        P("row", "col", None),
        P("row", "col", None, "lag"),
        P("row", "col", None, "lag", None, None),
        P(("row", "col", "lag"), None),
        P(("row", "col", "lag"), None, None),
    )
    out_specs = P(("row", "col", "lag"), None)
    step = functools.partial(per_device, mesh.shape["row"], mesh.shape["col"], mesh.shape["lag"])
    return jax.shard_map(step, mesh=mesh, in_specs=in_specs, out_specs=out_specs, check_vma=False)
```
